32 devices in a mesh: dp: 4 (over y, core), mp: 8 (over z, x).
Axes of the slice: x: 2, y: 2, z: 4, core: 2. Of those that a mesh axis runs over, the one named last changes fastest.
Arguments:
- inputs: bfloat16 [768, 32768], P('mp', 'dp'), may hold values from -6 to 6
- cotangent: bfloat16 [768, 32768], P('mp', 'dp'), may hold values from -5 to 5
- lengths: int32 [128], P('dp'), may hold values from 32 to 512, as said below
- vectors: float32 [5, 768], P(None, 'mp'), may hold values from -1 to 2
- hidden_bias: float32 [3072], P('mp'), may hold values from -2 to 2
- w_in: float32 [768, 3072], P(None, 'mp'), may hold values from -1 to 1
- w_out: float32 [3072, 768], P('mp'), may hold values from -1 to 1
- vec_first: float32 [5, 768], P(None, 'mp'), may hold values from -0.015625 to 0.015625
- vec_second: float32 [5, 768], P(None, 'mp'), may hold values from 9.536743e-07 to 3.8146973e-06
- bias_first: float32 [3072], P('mp'), may hold values from -0.0048828125 to 0.0048828125
- bias_second: float32 [3072], P('mp'), may hold values from 1.05963814e-07 to 4.2385525e-07
- in_first: float32 [768, 3072], P(None, 'mp'), may hold values from -0.0048828125 to 0.0048828125
- in_second: float32 [768, 3072], P(None, 'mp'), may hold values from 1.05963814e-07 to 4.2385525e-07
- out_first: float32 [3072, 768], P('mp'), may hold values from -0.009765625 to 0.009765625
- out_second: float32 [3072, 768], P('mp'), may hold values from 4.2385525e-07 to 1.695421e-06
Outputs:
- layer_out: bfloat16 [768, 32768], P('mp', 'dp')
- input_grad: float32 [768, 32768], P('mp', 'dp')
- grad_norm: float32 [], replicated
- vec_first_new: float32 [5, 768], P(None, 'mp')
- vec_second_new: float32 [5, 768], P(None, 'mp')
- vec_weight_new: float32 [5, 768], P(None, 'mp')
- bias_first_new: float32 [3072], P('mp')
- bias_second_new: float32 [3072], P('mp')
- bias_weight_new: float32 [3072], P('mp')
- in_first_new: float32 [768, 3072], P(None, 'mp')
- in_second_new: float32 [768, 3072], P(None, 'mp')
- in_weight_new: float32 [768, 3072], P(None, 'mp')
- out_first_new: float32 [3072, 768], P('mp')
- out_second_new: float32 [3072, 768], P('mp')
- out_weight_new: float32 [3072, 768], P('mp')
The draws below stay inside these ranges and needn't reach their ends.
Inputs may be any that keep to these rules, and one draw needn't show every extreme that they name: `lengths`: A sequence of L slots has L // 4 to L valid tokens; the first sequence of each bucket in each group is full.
All inputs are finite; a program needn't handle non-finite values.
Results may differ from the reference program's by a relative error of at most 0.015.
Values may be sent and summed in bfloat16 or wider, within the bound.
A program may use at most 256 MiB of HBM per device.

```python
import math
import jax
import jax.numpy as jnp
from jax import lax

D = 768
FF = 3072
UNITS = 8
LONG_LEN = 512
MID_LEN = 256
SHORT_LEN = 128
STEP = 3
GROUP_TOK = 8192
TOKENS = 32768
SEQS_ALL = 128
N_DP = 4


def rising(number, begin_value, end_value):
    fraction = jnp.arange(number, dtype=jnp.float32) / (number - 1)
    return begin_value + (end_value - begin_value) * fraction


def draw_lengths(key, part):
    key = jax.random.fold_in(key, 11)
    groups = SEQS_ALL // (4 * UNITS)
    slot_sizes = jnp.concatenate([jnp.full((UNITS,), LONG_LEN, jnp.int32), jnp.full((UNITS,), MID_LEN, jnp.int32), jnp.full((2 * UNITS,), SHORT_LEN, jnp.int32)])
    lowest = slot_sizes // 4
    raw_draw = jax.random.randint(key, (groups, 4 * UNITS), 0, 1 << 20)
    sampled = lowest[None, :] + raw_draw % (slot_sizes - lowest + 1)[None, :]
    bucket_heads = jnp.zeros((4 * UNITS,), jnp.int32).at[0].set(1).at[UNITS].set(1).at[2 * UNITS].set(1)
    sampled = jnp.where(bucket_heads[None, :] == 1, slot_sizes[None, :], sampled)
    return sampled.reshape(groups * 4 * UNITS).astype(jnp.int32)


def draw_inputs(key, part):
    key = jax.random.fold_in(key, 12)
    values = jnp.clip(jax.random.normal(key, (D, TOKENS), jnp.float32), -4.0, 4.0)
    scaling = rising(D, 0.65, 1.2)
    return (values * scaling[:, None]).astype(jnp.bfloat16)


def draw_vectors(key, part):
    key = jax.random.fold_in(key, 13)
    jitter = jnp.clip(jax.random.normal(key, (5, D), jnp.float32), -3.0, 3.0)
    gain_rise = rising(D, 0.6, 1.2)
    spread = 0.3
    gain_first = gain_rise * (1.0 + 0.08 * jitter[0])
    gain_second = gain_rise * (1.0 + 0.08 * jitter[2])
    return jnp.stack([gain_first, spread * jitter[1], gain_second, spread * jitter[3], spread * jitter[4]])


def draw_w_in(key, part):
    key = jax.random.fold_in(key, 14)
    values = jnp.clip(jax.random.normal(key, (D, FF), jnp.float32), -4.0, 4.0)
    scaling = rising(FF, 0.7, 1.25)
    return values * scaling[None, :] / math.sqrt(D)


def draw_w_out(key, part):
    key = jax.random.fold_in(key, 15)
    values = jnp.clip(jax.random.normal(key, (FF, D), jnp.float32), -4.0, 4.0)
    scaling = rising(FF, 0.7, 1.25)
    return values * scaling[:, None] / math.sqrt(FF)


def level_of(own_key, shape, cuts, smallest, high):
    def one(axis_at, parts):
        heights = jax.random.uniform(jax.random.fold_in(jax.random.fold_in(own_key, 6), axis_at), (parts,), jnp.float32, smallest / len(cuts), high / len(cuts))
        return jnp.repeat(jnp.exp(heights), shape[axis_at] // parts).reshape((-1,) + (1,) * (len(shape) - axis_at - 1))

    loudness = one(*cuts[0])
    for cut in cuts[1:]:
        loudness = loudness * one(*cut)
    return loudness


def scatter_about(own_key, shape, scale, most, cuts=(), kind=jnp.bfloat16):
    values = jax.random.normal(own_key, shape, jnp.float32) * scale
    if len(cuts) > 0:
        values = level_of(own_key, shape, cuts, -0.22, 0.18) * values
    return jnp.clip(values, min=-most, max=most).astype(kind)


def setup_inputs(seed: int = 0) -> dict:
    keys = jax.random.split(jax.random.key(seed), 16)
    return {
        "inputs": draw_inputs(jax.random.fold_in(keys[15], 71), 0),
        "cotangent": scatter_about(keys[1], (D, TOKENS), 1.0, 5.0, ((0, 8), (1, 4))),
        "lengths": draw_lengths(jax.random.fold_in(keys[15], 71), 0),
        "vectors": draw_vectors(jax.random.fold_in(keys[15], 71), 0),
        "hidden_bias": scatter_about(keys[4], (FF,), 0.5, 2.0, ((0, 8),), jnp.float32),
        "w_in": draw_w_in(jax.random.fold_in(keys[15], 71), 0),
        "w_out": draw_w_out(jax.random.fold_in(keys[15], 71), 0),
        "vec_first": scatter_about(keys[7], (5, D), (1.5 * (D * FF) ** -0.5), 0.015625, ((1, 8),), jnp.float32),
        "vec_second": jnp.clip(jnp.exp(math.log(3.814697265625e-06) - 1.3862944 * jax.random.uniform(keys[8], (5, D), jnp.float32) ** level_of(keys[8], (5, D), ((1, 8),), -0.2, 0.2)), 9.5367431640625e-07, 3.814697265625e-06),
        "bias_first": scatter_about(keys[9], (FF,), (0.5 * (D * FF) ** -0.5), 0.0048828125, ((0, 8),), jnp.float32),
        "bias_second": jnp.clip(jnp.exp(math.log(4.238552548940788e-07) - 1.3862944 * jax.random.uniform(keys[10], (FF,), jnp.float32) ** level_of(keys[10], (FF,), ((0, 8),), -0.2, 0.2)), 1.059638137235197e-07, 4.238552548940788e-07),
        "in_first": scatter_about(keys[11], (D, FF), (0.5 * (D * FF) ** -0.5), 0.0048828125, ((1, 8),), jnp.float32),
        "in_second": jnp.clip(jnp.exp(math.log(4.238552548940788e-07) - 1.3862944 * jax.random.uniform(keys[12], (D, FF), jnp.float32) ** level_of(keys[12], (D, FF), ((1, 8),), -0.2, 0.2)), 1.059638137235197e-07, 4.238552548940788e-07),
        "out_first": scatter_about(keys[13], (FF, D), (1.0 * (D * FF) ** -0.5), 0.009765625, ((0, 8),), jnp.float32),
        "out_second": jnp.clip(jnp.exp(math.log(1.6954210195763153e-06) - 1.3862944 * jax.random.uniform(keys[14], (FF, D), jnp.float32) ** level_of(keys[14], (FF, D), ((0, 8),), -0.2, 0.2)), 4.238552548940788e-07, 1.6954210195763153e-06),
    }


EPS_NORM = 1e-05
EPS_ADAM = 1e-08
BETA_ONE = 0.5
BETA_TWO = 0.5
CLIP_LIMIT = 1.0
DECAY_RATE = 0.01
RATE_IN = 0.03
RATE_OUT = 0.015
RATE_SMALL = 0.2

@jax.custom_vjp
def low(v):
    return lax.optimization_barrier(v.astype(jnp.bfloat16)).astype(jnp.float32)

@jax.custom_vjp
def low_back(v):
    return v

def low_keep(v):
    return (low(v), None)

def low_pass(kept, grad):
    return (grad,)

def back_keep(v):
    return (v, None)

def back_low(kept, grad):
    return (low(grad),)
low.defvjp(low_keep, low_pass)
low_back.defvjp(back_keep, back_low)

def exact_dot(left, right):
    return jnp.dot(left, right, precision=lax.Precision.HIGHEST, preferred_element_type=jnp.float32)

def buckets():
    return ((LONG_LEN, UNITS), (MID_LEN, UNITS), (SHORT_LEN, 2 * UNITS))

def full_tables(length):
    indices = jnp.arange(length, dtype=jnp.int32)
    product = indices[:, None] * indices[None, :] % length
    angles = product.astype(jnp.float32) * (2.0 * math.pi / length)
    scaling = 1.0 / math.sqrt(length)
    return (low(jnp.cos(angles) * scaling), low(jnp.sin(angles) * scaling))

def valid_tokens(lengths):
    pieces = []
    first_slot = 0
    for length, number in buckets():
        position = jnp.arange(length, dtype=jnp.int32)
        chosen = lengths[first_slot:first_slot + number]
        pieces.append((position[None, :] < chosen[:, None]).astype(jnp.float32).reshape(number * length))
        first_slot += number
    return jnp.concatenate(pieces)

def sequence_mix(part_a, part_b):
    pieces = []
    offset = 0
    for length, number in buckets():
        cos_tab, sin_tab = full_tables(length)
        extent = length * number
        block_a = part_a[:, offset:offset + extent].reshape(D, number, length)
        block_b = part_b[:, offset:offset + extent].reshape(D, number, length)
        mixed_rows = jnp.einsum('dun,mn->dum', block_a, cos_tab, precision=lax.Precision.HIGHEST) - jnp.einsum('dun,mn->dum', block_b, sin_tab, precision=lax.Precision.HIGHEST)
        pieces.append(mixed_rows.reshape(D, extent))
        offset += extent
    return jnp.concatenate(pieces, axis=1)

def layer_norm(values, gain, shift):
    mean_val = lax.optimization_barrier(jnp.mean(values, axis=0, keepdims=True))
    centred = values - mean_val
    variance = lax.optimization_barrier(jnp.mean(centred * centred, axis=0, keepdims=True))
    return centred * lax.rsqrt(variance + EPS_NORM) * gain[:, None] + shift[:, None]

def exact_gelu(values):
    return jax.nn.gelu(values, approximate=False)

def group_forward(inputs_g, valid_g, vectors, hidden_bias, w_in_low, w_out_low):
    cos_d, sin_d = full_tables(D)
    masked = low(inputs_g * valid_g[None, :])
    part_a = low_back(low(exact_dot(cos_d, masked)))
    part_b = low_back(low(exact_dot(sin_d, masked)))
    mixed_rows = low_back(sequence_mix(part_a, part_b))
    first_res = inputs_g + mixed_rows
    hidden = layer_norm(first_res, vectors[0], vectors[1])
    pre_act = low_back(exact_dot(w_in_low.T, low(hidden))) + hidden_bias[:, None]
    activated = low(exact_gelu(pre_act))
    down_part = low_back(exact_dot(w_out_low.T, activated)) + vectors[4][:, None]
    return layer_norm(hidden + down_part, vectors[2], vectors[3])

def layer_forward(inputs_f, vectors, hidden_bias, w_in, w_out, valid):
    w_in_low = low(w_in)
    w_out_low = low(w_out)
    grouped = inputs_f.reshape(D, N_DP, GROUP_TOK).transpose(1, 0, 2)
    valid_grouped = valid.reshape(N_DP, GROUP_TOK)

    def one_group(carried):
        return group_forward(carried[0], carried[1], vectors, hidden_bias, w_in_low, w_out_low)
    outputs = lax.map(jax.checkpoint(one_group), (grouped, valid_grouped))
    return outputs.transpose(1, 0, 2).reshape(D, N_DP * GROUP_TOK)

def adam_step(weight, grad, first_old, second_old, factor, rate, decay):
    clipped = grad * factor
    first_new = BETA_ONE * first_old + (1.0 - BETA_ONE) * clipped
    second_new = BETA_TWO * second_old + (1.0 - BETA_TWO) * clipped * clipped
    first_hat = first_new / (1.0 - BETA_ONE ** STEP)
    second_hat = second_new / (1.0 - BETA_TWO ** STEP)
    weight_new = weight - rate * (first_hat / (jnp.sqrt(second_hat) + EPS_ADAM) + decay * weight)
    return (first_new, second_new, weight_new)

def reference(inputs, cotangent, lengths, vectors, hidden_bias, w_in, w_out, vec_first, vec_second, bias_first, bias_second, in_first, in_second, out_first, out_second):
    valid = jax.vmap(valid_tokens)(lengths.reshape(N_DP, 4 * UNITS)).reshape(N_DP * GROUP_TOK)
    inputs_f = inputs.astype(jnp.float32)

    def forward(inputs_v, vectors_v, bias_v, w_in_v, w_out_v):
        return layer_forward(inputs_v, vectors_v, bias_v, w_in_v, w_out_v, valid)
    outputs, pullback = jax.vjp(forward, inputs_f, vectors, hidden_bias, w_in, w_out)
    input_grad, grad_vec, grad_bias, grad_in, grad_out = pullback(cotangent.astype(jnp.float32))
    total_sq = jnp.sum(grad_vec * grad_vec) + jnp.sum(grad_bias * grad_bias) + jnp.sum(grad_in * grad_in) + jnp.sum(grad_out * grad_out)
    grad_norm = jnp.sqrt(total_sq)
    factor = CLIP_LIMIT / jnp.maximum(grad_norm, CLIP_LIMIT)
    vec_state = adam_step(vectors, grad_vec, vec_first, vec_second, factor, RATE_SMALL, 0.0)
    bias_state = adam_step(hidden_bias, grad_bias, bias_first, bias_second, factor, RATE_SMALL, 0.0)
    in_state = adam_step(w_in, grad_in, in_first, in_second, factor, RATE_IN, DECAY_RATE)
    out_state = adam_step(w_out, grad_out, out_first, out_second, factor, RATE_OUT, DECAY_RATE)
    return (outputs.astype(jnp.bfloat16), input_grad, grad_norm, vec_state[0], vec_state[1], vec_state[2], bias_state[0], bias_state[1], bias_state[2], in_state[0], in_state[1], in_state[2], out_state[0], out_state[1], out_state[2])
```

```python
import functools
import math

import jax
import jax.numpy as jnp
import numpy as np
from jax import lax
from jax.experimental import pallas as pl
from jax.experimental.pallas import tpu as pltpu
from jax.sharding import PartitionSpec as P

D = 768
UNITS = 8
LONG_LEN = 512
MID_LEN = 256
SHORT_LEN = 128
STEP = 3


EPS_NORM = 1e-05
EPS_ADAM = 1e-08
BETA_ONE = 0.5
BETA_TWO = 0.5
CLIP_LIMIT = 1.0
DECAY_RATE = 0.01
RATE_IN = 0.03
RATE_OUT = 0.015
RATE_SMALL = 0.2


def buckets():
    return ((LONG_LEN, UNITS), (MID_LEN, UNITS), (SHORT_LEN, 2 * UNITS))


def dft_block(rows_index, cols_index, length):
    product = rows_index[:, None] * cols_index[None, :] % length
    angles = product.astype(jnp.float32) * (2.0 * math.pi / length)
    scaling = 1.0 / math.sqrt(length)
    return (
        (jnp.cos(angles) * scaling).astype(jnp.bfloat16),
        (jnp.sin(angles) * scaling).astype(jnp.bfloat16),
    )


def bucket_table(length):
    indices = jnp.arange(length, dtype=jnp.int32)
    cos_tab, sin_tab = dft_block(indices, indices, length)
    return jnp.concatenate([cos_tab, -sin_tab], axis=1)


def valid_tokens(lengths):
    pieces = []
    first_slot = 0
    for length, number in buckets():
        position = jnp.arange(length, dtype=jnp.int32)
        chosen = lengths[first_slot : first_slot + number]
        pieces.append(
            (position[None, :] < chosen[:, None]).astype(jnp.float32).reshape(number * length)
        )
        first_slot += number
    return jnp.concatenate(pieces)


def sequence_mix(part_a, part_b):
    pieces = []
    offset = 0
    for length, number in buckets():
        stacked_tab = bucket_table(length)
        extent = length * number
        block_a = part_a[:, offset : offset + extent].reshape(-1, number, length)
        block_b = part_b[:, offset : offset + extent].reshape(-1, number, length)
        joined = jnp.concatenate([block_a, block_b], axis=2)
        mixed_rows = jnp.einsum(
            "dun,mn->dum", joined, stacked_tab, preferred_element_type=jnp.float32
        )
        pieces.append(mixed_rows.reshape(-1, extent))
        offset += extent
    return jnp.concatenate(pieces, axis=1)


def sequence_unmix(grad_low):
    pieces_a = []
    pieces_b = []
    offset = 0
    for length, number in buckets():
        stacked_tab = bucket_table(length)
        extent = length * number
        sliced = grad_low[:, offset : offset + extent].reshape(-1, number, length)
        joined = jnp.einsum("dum,mn->dun", sliced, stacked_tab, preferred_element_type=jnp.float32)
        pieces_a.append(joined[:, :, :length].reshape(-1, extent))
        pieces_b.append(joined[:, :, length:].reshape(-1, extent))
        offset += extent
    return (jnp.concatenate(pieces_a, axis=1), jnp.concatenate(pieces_b, axis=1))


def normalize(values, row_sum, row_sq):
    mean_val = row_sum / D
    variance = row_sq / D - mean_val * mean_val
    scaling = lax.rsqrt(variance + EPS_NORM)[None, :]
    return ((values - mean_val[None, :]) * scaling, scaling)


def exact_gelu(values):
    return jax.nn.gelu(values, approximate=False)


def adam_step(weight, grad, first_old, second_old, factor, rate, decay):
    clipped = grad * factor
    first_new = BETA_ONE * first_old + (1.0 - BETA_ONE) * clipped
    second_new = BETA_TWO * second_old + (1.0 - BETA_TWO) * clipped * clipped
    first_hat = first_new / (1.0 - BETA_ONE**STEP)
    second_hat = second_new / (1.0 - BETA_TWO**STEP)
    weight_new = weight - rate * (first_hat / (jnp.sqrt(second_hat) + EPS_ADAM) + decay * weight)
    return (first_new, second_new, weight_new)


def shards(
    inputs,
    cotangent,
    lengths,
    vectors,
    hidden_bias,
    w_in,
    w_out,
    vec_first,
    vec_second,
    bias_first,
    bias_second,
    in_first,
    in_second,
    out_first,
    out_second,
):
    width_local = inputs.shape[0]
    group_tok = inputs.shape[1]
    feat_index = lax.axis_index("mp") * width_local + jnp.arange(width_local, dtype=jnp.int32)
    contract_first = (((0,), (0,)), ((), ()))
    contract_last = (((1,), (1,)), ((), ()))
    valid = valid_tokens(lengths)
    inputs_f = inputs.astype(jnp.float32)
    masked = (inputs_f * valid[None, :]).astype(jnp.bfloat16)
    rows_index = jnp.arange(width_local * lax.axis_size("mp"), dtype=jnp.int32)
    cos_tab, sin_tab = dft_block(rows_index, feat_index, D)
    both_parts = lax.psum_scatter(
        jnp.concatenate(
            [
                jnp.dot(cos_tab, masked, preferred_element_type=jnp.float32),
                jnp.dot(sin_tab, masked, preferred_element_type=jnp.float32),
            ],
            axis=1,
        ),
        "mp",
        scatter_dimension=0,
        tiled=True,
    )
    part_a = both_parts[:, :group_tok].astype(jnp.bfloat16)
    part_b = both_parts[:, group_tok:].astype(jnp.bfloat16)
    mixed_rows = sequence_mix(part_a, part_b)
    first_res = inputs_f + mixed_rows
    first_sum, first_sq = (
        lax.psum(jnp.sum(first_res, axis=0).astype(jnp.bfloat16), "mp").astype(jnp.float32),
        lax.psum(jnp.sum(first_res * first_res, axis=0).astype(jnp.bfloat16), "mp").astype(
            jnp.float32
        ),
    )
    first_hat, first_scale = normalize(first_res, first_sum, first_sq)
    hidden = first_hat * vectors[0][:, None] + vectors[1][:, None]
    hidden_low = hidden.astype(jnp.bfloat16)
    hidden_all = lax.all_gather(hidden_low, "mp", axis=0, tiled=True)
    w_in_low = w_in.astype(jnp.bfloat16)
    w_out_low = w_out.astype(jnp.bfloat16)
    pre_act = (
        lax.dot_general(w_in_low, hidden_all, contract_first, preferred_element_type=jnp.float32)
        + hidden_bias[:, None]
    )
    activ_f, gelu_back = jax.vjp(exact_gelu, pre_act)
    activated = activ_f.astype(jnp.bfloat16)
    columns = w_out_low
    down_part = lax.psum_scatter(
        lax.dot_general(
            columns, activated, contract_first, preferred_element_type=jnp.float32
        ).astype(jnp.bfloat16),
        "mp",
        scatter_dimension=0,
        tiled=True,
    ).astype(jnp.float32)
    second_res = hidden + down_part + vectors[4][:, None]
    second_sum, second_sq = (
        lax.psum(jnp.sum(second_res, axis=0).astype(jnp.bfloat16), "mp").astype(jnp.float32),
        lax.psum(jnp.sum(second_res * second_res, axis=0).astype(jnp.bfloat16), "mp").astype(
            jnp.float32
        ),
    )
    second_hat, second_scale = normalize(second_res, second_sum, second_sq)
    layer_out = (second_hat * vectors[2][:, None] + vectors[3][:, None]).astype(jnp.bfloat16)
    out_grad = cotangent.astype(jnp.float32)
    grad_gain_two = jnp.sum(out_grad * second_hat, axis=1)
    grad_shift_two = jnp.sum(out_grad, axis=1)
    scaled_two = out_grad * vectors[2][:, None]
    back_sum, back_dot = (
        lax.psum(jnp.sum(scaled_two, axis=0).astype(jnp.bfloat16), "mp").astype(jnp.float32),
        lax.psum(jnp.sum(scaled_two * second_hat, axis=0).astype(jnp.bfloat16), "mp").astype(
            jnp.float32
        ),
    )
    second_grad = second_scale * (
        scaled_two - back_sum[None, :] / D - second_hat * back_dot[None, :] / D
    )
    grad_out_bias = jnp.sum(second_grad, axis=1)
    second_low = second_grad.astype(jnp.bfloat16)
    row_block = lax.all_gather(second_low, "mp", axis=0, tiled=True)
    columns = w_out_low
    act_grad = jnp.dot(columns, row_block, preferred_element_type=jnp.float32)
    block_grad = lax.dot_general(
        activated, row_block, contract_last, preferred_element_type=jnp.float32
    )
    act_grad, grad_out = (act_grad, block_grad)
    pre_grad = gelu_back(act_grad)[0]
    grad_bias = jnp.sum(pre_grad, axis=1)
    pre_low = pre_grad.astype(jnp.bfloat16)
    grad_in = lax.dot_general(
        hidden_all, pre_low, contract_last, preferred_element_type=jnp.float32
    )
    row_block = w_in_low
    hidden_grad = (
        lax.psum_scatter(
            jnp.dot(row_block, pre_low, preferred_element_type=jnp.float32).astype(jnp.bfloat16),
            "mp",
            scatter_dimension=0,
            tiled=True,
        ).astype(jnp.float32)
        + second_grad
    )
    grad_gain_one = jnp.sum(hidden_grad * first_hat, axis=1)
    grad_shift_one = jnp.sum(hidden_grad, axis=1)
    scaled_one = hidden_grad * vectors[0][:, None]
    sum_one, dot_one = (
        lax.psum(jnp.sum(scaled_one, axis=0).astype(jnp.bfloat16), "mp").astype(jnp.float32),
        lax.psum(jnp.sum(scaled_one * first_hat, axis=0).astype(jnp.bfloat16), "mp").astype(
            jnp.float32
        ),
    )
    first_grad = first_scale * (
        scaled_one - sum_one[None, :] / D - first_hat * dot_one[None, :] / D
    )
    grad_a_f, grad_b_f = sequence_unmix(first_grad.astype(jnp.bfloat16))
    grad_a = grad_a_f.astype(jnp.bfloat16)
    grad_b = grad_b_f.astype(jnp.bfloat16)
    cols_index = jnp.arange(lax.axis_size("mp") * width_local, dtype=jnp.int32)
    cos_tab, sin_tab = dft_block(feat_index, cols_index, D)
    masked_grad = lax.psum_scatter(
        (
            lax.dot_general(cos_tab, grad_a, contract_first, preferred_element_type=jnp.float32)
            + lax.dot_general(sin_tab, grad_b, contract_first, preferred_element_type=jnp.float32)
        ).astype(jnp.bfloat16),
        "mp",
        scatter_dimension=0,
        tiled=True,
    ).astype(jnp.float32)
    input_grad = first_grad + valid[None, :] * masked_grad
    grad_vec = jnp.stack(
        [grad_gain_one, grad_shift_one, grad_gain_two, grad_shift_two, grad_out_bias]
    )
    grad_vec, grad_bias, grad_in, grad_out = (
        lax.psum(grad_vec.astype(jnp.bfloat16), "dp").astype(jnp.float32),
        lax.psum(grad_bias.astype(jnp.bfloat16), "dp").astype(jnp.float32),
        lax.psum(grad_in.astype(jnp.bfloat16), "dp").astype(jnp.float32),
        lax.psum(grad_out.astype(jnp.bfloat16), "dp").astype(jnp.float32),
    )
    squares = (
        jnp.sum(grad_vec * grad_vec)
        + jnp.sum(grad_bias * grad_bias)
        + jnp.sum(grad_in * grad_in)
        + jnp.sum(grad_out * grad_out)
    )
    total_sq = lax.psum(squares, "mp")
    grad_norm = jnp.sqrt(total_sq)
    factor = CLIP_LIMIT / jnp.maximum(grad_norm, CLIP_LIMIT)
    vec_state = adam_step(vectors, grad_vec, vec_first, vec_second, factor, RATE_SMALL, 0.0)
    bias_state = adam_step(hidden_bias, grad_bias, bias_first, bias_second, factor, RATE_SMALL, 0.0)
    in_state = adam_step(w_in, grad_in, in_first, in_second, factor, RATE_IN, DECAY_RATE)
    out_state = adam_step(w_out, grad_out, out_first, out_second, factor, RATE_OUT, DECAY_RATE)
    return (
        layer_out,
        input_grad,
        grad_norm,
        vec_state[0],
        vec_state[1],
        vec_state[2],
        bias_state[0],
        bias_state[1],
        bias_state[2],
        in_state[0],
        in_state[1],
        in_state[2],
        out_state[0],
        out_state[1],
        out_state[2],
    )


N_MP = 8
N_DP = 4
FF = 3072
SHARD = D // N_MP
UNIT = FF // N_MP
TOK = LONG_LEN + MID_LEN + 2 * SHORT_LEN
HALF = TOK // 2
QUARTER = UNIT // N_DP
ROWS_IN = D // N_DP
VMEM_LIMIT = 60 * 1024 * 1024
SLOTS = (
    ((UNITS * LONG_LEN, MID_LEN, 0), (UNITS * (LONG_LEN + MID_LEN), 2 * SHORT_LEN, MID_LEN)),
    ((0, LONG_LEN, HALF),),
)


def table(length):
    index = np.arange(length, dtype=np.int64)
    angles = ((index[:, None] * index[None, :]) % length).astype(np.float32) * np.float32(
        2.0 * math.pi / length
    )
    scaling = np.float32(1.0 / math.sqrt(length))
    return (
        (np.cos(angles).astype(np.float32) * scaling).astype(jnp.bfloat16),
        (np.sin(angles).astype(np.float32) * scaling).astype(jnp.bfloat16),
    )


def place():
    mp = lax.axis_index("mp")
    dp = lax.axis_index("dp")
    return mp, dp, mp // 2, mp % 2, dp // 2, dp % 2


def barrier():
    mp, dp = lax.axis_index("mp"), lax.axis_index("dp")
    sem = pltpu.get_barrier_semaphore()
    for step in range(1, N_MP):
        pl.semaphore_signal(sem, inc=1, device_id={"mp": (mp + step) % N_MP})
    for step in range(1, N_DP):
        pl.semaphore_signal(sem, inc=1, device_id={"dp": (dp + step) % N_DP})
    pl.semaphore_wait(sem, N_MP + N_DP - 2)


def wait_bytes(ref, sem):
    pltpu.make_async_copy(ref, ref, sem).wait()


def rows96(index):
    return pl.ds(pl.multiple_of(index * SHARD, 32), SHARD)


def spread_in(source, target, half, send_sem, recv_sem, own_sem):
    mp = lax.axis_index("mp")
    for offset, width, local in SLOTS[half]:
        for step in range(1, N_MP):
            peer = (mp + step) % N_MP
            pltpu.make_async_remote_copy(
                source.at[:, pl.ds(pl.multiple_of(offset + width * peer, 256), width)],
                target.at[rows96(mp), pl.ds(local, width)],
                send_sem,
                recv_sem,
                device_id={"mp": peer},
            ).start()
        pltpu.make_async_copy(
            source.at[:, pl.ds(pl.multiple_of(offset + width * mp, 256), width)],
            target.at[rows96(mp), pl.ds(local, width)],
            own_sem,
        ).start()


def spread_out(source, target, half, send_sem, recv_sem, own_sem):
    mp = lax.axis_index("mp")
    for offset, width, local in SLOTS[half]:
        columns = pl.ds(pl.multiple_of(offset + width * mp, 256), width)
        for step in range(1, N_MP):
            peer = (mp + step) % N_MP
            pltpu.make_async_remote_copy(
                source.at[rows96(peer), pl.ds(local, width)],
                target.at[:, columns],
                send_sem,
                recv_sem,
                device_id={"mp": peer},
            ).start()
        pltpu.make_async_copy(
            source.at[rows96(mp), pl.ds(local, width)], target.at[:, columns], own_sem
        ).start()


def region(ref, kind, mp, dp):
    if kind == 0:
        return ref.at[
            pl.ds(pl.multiple_of(dp * ROWS_IN, 64), ROWS_IN),
            pl.ds(pl.multiple_of(mp * UNIT, 128), UNIT),
        ]
    return ref.at[pl.ds(pl.multiple_of(mp * UNIT + dp * QUARTER, 32), QUARTER), :]


def push(ref, kind, mp, dp, target, send_sem, recv_sem):
    part = region(ref, kind, mp, dp)
    return pltpu.make_async_remote_copy(
        part, part, send_sem.at[kind], recv_sem.at[kind, mp * N_DP + dp], device_id=target
    )


def gather_steps(ref, kind, send_sem, recv_sem):
    mp, dp, z, x, y, c = place()

    def send(mp_from, dp_from, target):
        push(ref, kind, mp_from, dp_from, target, send_sem, recv_sem).start()

    def wait(mp_from, dp_from):
        push(ref, kind, mp_from, dp_from, {"mp": mp}, send_sem, recv_sem).wait_recv()

    to_x = {"mp": 2 * z + 1 - x}
    to_y = {"dp": 2 * (1 - y) + c}
    to_c = {"dp": 2 * y + 1 - c}

    def along_z():
        for step in range(1, 4):
            send(mp, dp, {"mp": 2 * ((z + step) % 4) + x})

    def second():
        if kind == 0:
            send(mp, dp, to_x)
        else:
            send(mp, dp, to_x)
            send(mp, 2 * (1 - y) + c, to_x)
        for step in range(1, 4):
            other = 2 * ((z + step) % 4) + x
            wait(other, dp)
            send(other, dp, to_x if kind == 0 else to_y)
            if kind == 0:
                send(other, dp, to_y)
            else:
                send(other, dp, to_x)

    def third():
        if kind == 0:
            for step in range(4):
                other = 2 * ((z + step) % 4) + 1 - x
                wait(other, dp)
                send(other, dp, to_y)
        else:
            for step in range(1, 4):
                other = 2 * ((z + step) % 4) + x
                wait(other, 2 * (1 - y) + c)
                send(other, 2 * (1 - y) + c, to_x)

    def fourth():
        for step in range(1, 4):
            other = 2 * ((z + step) % 4) + x
            send(other, dp, to_c)
        if kind == 0:
            for step in range(4):
                send(2 * ((z + step) % 4) + 1 - x, dp, to_c)
            for step in range(1, N_MP):
                other = (mp + step) % N_MP
                wait(other, 2 * (1 - y) + c)
                send(other, 2 * (1 - y) + c, to_c)
        else:
            for step in range(1, 4):
                send(2 * ((z + step) % 4) + x, 2 * (1 - y) + c, to_c)
            for half in (y, 1 - y):
                for step in range(4):
                    other = 2 * ((z + step) % 4) + 1 - x
                    wait(other, 2 * half + c)
                    send(other, 2 * half + c, to_c)

    def fifth():
        for half in (0, 1):
            for step in range(1, N_MP):
                wait((mp + step) % N_MP, 2 * half + 1 - c)

    return along_z, second, third, fourth, fifth


def gather_kernel(
    x_ref, cot_ref, in_ref, out_ref, small_ref,
    x_all, cot_all, in_all, out_all, small_all,
    send, recv, own, w_send, w_recv,
):
    mp = lax.axis_index("mp")
    barrier()
    in_steps = gather_steps(in_all, 0, w_send, w_recv)
    out_steps = gather_steps(out_all, 1, w_send, w_recv)
    shard_in = pltpu.make_async_copy(
        in_ref, in_all.at[:, pl.ds(pl.multiple_of(mp * UNIT, 128), UNIT)], own.at[5]
    )
    shard_out = pltpu.make_async_copy(
        out_ref, out_all.at[pl.ds(pl.multiple_of(mp * UNIT, 128), UNIT), :], own.at[6]
    )
    shard_in.start()
    shard_out.start()
    spread_in(x_ref, x_all, 0, send.at[0], recv.at[0], own.at[0])
    shard_in.wait()
    in_steps[0]()
    shard_out.wait()
    out_steps[0]()
    spread_in(x_ref, x_all, 1, send.at[1], recv.at[1], own.at[1])
    for step in range(1, N_MP):
        pltpu.make_async_remote_copy(
            small_ref, small_all.at[mp], send.at[4], recv.at[4], device_id={"mp": (mp + step) % N_MP}
        ).start()
    pltpu.make_async_copy(small_ref, small_all.at[mp], own.at[4]).start()
    for stage in range(1, 5):
        in_steps[stage]()
        out_steps[stage]()
        if stage == 1:
            spread_in(cot_ref, cot_all, 0, send.at[2], recv.at[2], own.at[2])
            spread_in(cot_ref, cot_all, 1, send.at[3], recv.at[3], own.at[3])
    for half in range(2):
        for slot, ref in ((half, x_all), (2 + half, cot_all)):
            wait_bytes(ref.at[pl.ds(0, D - SHARD), pl.ds(HALF * half, HALF)], send.at[slot])
            wait_bytes(ref.at[pl.ds(0, D - SHARD), pl.ds(HALF * half, HALF)], recv.at[slot])
            wait_bytes(ref.at[pl.ds(0, SHARD), pl.ds(HALF * half, HALF)], own.at[slot])
    wait_bytes(small_all.at[pl.ds(0, N_MP - 1)], send.at[4])
    wait_bytes(small_all.at[pl.ds(0, N_MP - 1)], recv.at[4])
    wait_bytes(small_all.at[0], own.at[4])
    for kind in range(2):
        wait_bytes(out_all.at[pl.ds(0, 28 * QUARTER), :], w_send.at[kind])


def gather_all(inputs, cotangent, w_in_low, w_out_low, small):
    anywhere = pl.BlockSpec(memory_space=pl.ANY)
    return pl.pallas_call(
        gather_kernel,
        out_shape=(
            jax.ShapeDtypeStruct((D, TOK), jnp.bfloat16),
            jax.ShapeDtypeStruct((D, TOK), jnp.bfloat16),
            jax.ShapeDtypeStruct((D, FF), jnp.bfloat16),
            jax.ShapeDtypeStruct((FF, D), jnp.bfloat16),
            jax.ShapeDtypeStruct((N_MP,) + small.shape, jnp.float32),
        ),
        in_specs=[anywhere] * 5,
        out_specs=(anywhere,) * 5,
        scratch_shapes=[
            pltpu.SemaphoreType.DMA((5,)),
            pltpu.SemaphoreType.DMA((5,)),
            pltpu.SemaphoreType.DMA((7,)),
            pltpu.SemaphoreType.DMA((2,)),
            pltpu.SemaphoreType.DMA((2, N_MP * N_DP)),
        ],
        compiler_params=pltpu.CompilerParams(
            collective_id=0, has_side_effects=True, vmem_limit_bytes=VMEM_LIMIT
        ),
    )(inputs, cotangent, w_in_low, w_out_low, small)


def add_into(ref, left, right):
    ref[...] = (left.astype(jnp.float32) + right.astype(jnp.float32)).astype(ref.dtype)


def reduce_steps(grad, kind, core_buf, second_buf, third_buf, last_buf, final, send, recv):
    mp, dp, z, x, y, c = place()
    to_x = {"mp": 2 * z + 1 - x}
    to_y = {"dp": 2 * (1 - y) + c}
    to_c = {"dp": 2 * y + 1 - c}

    def copy(stage, piece, source, target, device):
        return pltpu.make_async_remote_copy(
            source, target, send.at[kind, stage], recv.at[kind, stage, piece], device_id=device
        )

    def core(step):
        piece = (z + 1 + step) % 4
        return copy(0, step, grad.at[piece, :, :, 1 - c], core_buf.at[piece], to_c)

    def second(step):
        piece = (z + 1 + step) % 4
        if kind == 0:
            return copy(1, step, core_buf.at[piece, 1 - x], second_buf.at[piece], to_x)
        return copy(1, step, core_buf.at[piece, :, 1 - y], second_buf.at[piece], to_y)

    def third(step):
        piece = (z + 1 + step) % 4
        if kind == 0:
            return copy(2, step, second_buf.at[piece, 1 - y], third_buf.at[piece], to_y)
        return copy(2, step, second_buf.at[piece, 1 - x], third_buf.at[piece], to_x)

    def last(step):
        piece = (z + 1 + step) % 4
        return copy(3, step, third_buf.at[piece], last_buf.at[2 - step], {"mp": 2 * piece + x})

    def start(step):
        core(step).start()

    def after_core(step):
        piece = (z + 1 + step) % 4
        core(step).wait_recv()
        add_into(core_buf.at[piece], core_buf[piece], grad[piece, :, :, c])
        second(step).start()

    def after_second(step):
        piece = (z + 1 + step) % 4
        second(step).wait_recv()
        mine = core_buf[piece, x] if kind == 0 else core_buf[piece, :, y]
        add_into(second_buf.at[piece], second_buf[piece], mine)
        third(step).start()

    def after_third(step):
        piece = (z + 1 + step) % 4
        third(step).wait_recv()
        mine = second_buf[piece, y] if kind == 0 else second_buf[piece, x]
        add_into(third_buf.at[piece], third_buf[piece], mine)
        if step < 3:
            last(step).start()

    def finish():
        total = third_buf[z].astype(jnp.float32)
        for slot in range(3):
            pltpu.make_async_remote_copy(
                third_buf.at[z], last_buf.at[slot], send.at[kind, 3], recv.at[kind, 3, 2 - slot],
                device_id={"mp": mp},
            ).wait_recv()
            total = total + last_buf[slot].astype(jnp.float32)
        final[dp] = total.astype(final.dtype)
        for step in range(1, N_DP):
            pltpu.make_async_remote_copy(
                final.at[dp], final.at[dp], send.at[kind, 4], recv.at[kind, 4, 3 - step],
                device_id={"dp": (dp + step) % N_DP},
            ).start()

    def collect():
        for step in range(1, N_DP):
            other = (dp + N_DP - step) % N_DP
            pltpu.make_async_remote_copy(
                final.at[other], final.at[other], send.at[kind, 4], recv.at[kind, 4, 3 - step],
                device_id={"mp": mp},
            ).wait_recv()

    def drain():
        wait_bytes(core_buf, send.at[kind, 0])
        wait_bytes(second_buf, send.at[kind, 1])
        wait_bytes(third_buf, send.at[kind, 2])
        wait_bytes(third_buf.at[pl.ds(0, 3)], send.at[kind, 3])
        wait_bytes(final.at[pl.ds(0, 3)], send.at[kind, 4])

    return start, after_core, after_second, after_third, finish, collect, drain


def scatter_kernel(
    layer_ref, back_ref, grad_in, grad_out,
    layer_all, back_all, final_in, final_out,
    core_in, core_out, second_in, second_out, third_in, third_out, last_in, last_out,
    send, recv, own, g_send, g_recv,
):
    barrier()
    outs = reduce_steps(
        grad_out, 1, core_out, second_out, third_out, last_out, final_out, g_send, g_recv
    )
    ins = reduce_steps(grad_in, 0, core_in, second_in, third_in, last_in, final_in, g_send, g_recv)
    for step in range(4):
        outs[0](step)
        ins[0](step)
    for half in range(2):
        spread_out(layer_ref, layer_all, half, send.at[half], recv.at[half], own.at[half])
    for half in range(2):
        spread_out(back_ref, back_all, half, send.at[2 + half], recv.at[2 + half], own.at[2 + half])
    for stage in range(1, 4):
        for step in range(4):
            outs[stage](step)
            ins[stage](step)
    for stage in range(4, 7):
        outs[stage]()
        ins[stage]()
    for slot, ref in ((0, layer_all), (1, layer_all), (2, back_all), (3, back_all)):
        wait_bytes(ref.at[:, pl.ds(0, 7 * HALF)], send.at[slot])
        wait_bytes(ref.at[:, pl.ds(0, 7 * HALF)], recv.at[slot])
        wait_bytes(ref.at[:, pl.ds(0, HALF)], own.at[slot])


def scatter_all(layer_out, back, grad_in, grad_out):
    anywhere = pl.BlockSpec(memory_space=pl.ANY)
    vmem = pl.BlockSpec(memory_space=pltpu.VMEM)
    tokens = N_MP * TOK
    pair = lambda shape: [pltpu.VMEM(shape, jnp.bfloat16)] * 2
    return pl.pallas_call(
        scatter_kernel,
        out_shape=(
            jax.ShapeDtypeStruct((SHARD, tokens), jnp.bfloat16),
            jax.ShapeDtypeStruct((SHARD, tokens), jnp.bfloat16),
            jax.ShapeDtypeStruct((N_DP, QUARTER, D), jnp.bfloat16),
            jax.ShapeDtypeStruct((N_DP, QUARTER, D), jnp.bfloat16),
        ),
        in_specs=[anywhere, anywhere, vmem, vmem],
        out_specs=(anywhere, anywhere, vmem, vmem),
        scratch_shapes=[
            *pair((4, 2, 2, QUARTER, D)),
            *pair((4, 2, QUARTER, D)),
            *pair((4, QUARTER, D)),
            *pair((3, QUARTER, D)),
            pltpu.SemaphoreType.DMA((4,)),
            pltpu.SemaphoreType.DMA((4,)),
            pltpu.SemaphoreType.DMA((4,)),
            pltpu.SemaphoreType.DMA((2, 5)),
            pltpu.SemaphoreType.DMA((2, 5, 4)),
        ],
        compiler_params=pltpu.CompilerParams(
            collective_id=1, has_side_effects=True, vmem_limit_bytes=VMEM_LIMIT
        ),
    )(layer_out, back, grad_in, grad_out)


def split_tables():
    cos_m, sin_m = table(MID_LEN)
    cos_s, sin_s = table(SHORT_LEN)
    cos_l, sin_l = table(LONG_LEN)
    zero = np.zeros_like(cos_s)
    cos_s = np.block([[cos_s, zero], [zero, cos_s]])
    sin_s = np.block([[sin_s, zero], [zero, sin_s]])
    return (
        (0, MID_LEN, cos_m, sin_m),
        (MID_LEN, 2 * SHORT_LEN, cos_s, sin_s),
        (HALF, LONG_LEN, cos_l, sin_l),
    )


def local_valid(lengths, mp):
    def one(length, first, number, chosen):
        position = jnp.arange(length, dtype=jnp.int32)
        local = lax.dynamic_slice(lengths, (first + number * mp,), (number,))
        return (position[None, :] < local[:, None]).astype(jnp.float32).reshape(-1)

    return jnp.concatenate(
        [
            one(MID_LEN, UNITS, 1, None),
            one(SHORT_LEN, 2 * UNITS, 2, None),
            one(LONG_LEN, 0, 1, None),
        ]
    )


def dot(left, right):
    return jnp.dot(left, right, preferred_element_type=jnp.float32)


def dot_tn(left, right):
    return lax.dot_general(left, right, (((0,), (0,)), ((), ())), preferred_element_type=jnp.float32)


def dot_nt(left, right):
    return lax.dot_general(left, right, (((1,), (1,)), ((), ())), preferred_element_type=jnp.float32)


def layer_norm(values):
    mean_val = jnp.mean(values, axis=0, keepdims=True)
    centred = values - mean_val
    scaling = lax.rsqrt(jnp.mean(centred * centred, axis=0, keepdims=True) + EPS_NORM)
    return centred * scaling, scaling


def norm_back(grad, hat, scaling):
    mean_grad = jnp.mean(grad, axis=0, keepdims=True)
    mean_dot = jnp.mean(grad * hat, axis=0, keepdims=True)
    return scaling * (grad - mean_grad - hat * mean_dot)


def token_shards(
    inputs,
    cotangent,
    lengths,
    vectors,
    hidden_bias,
    w_in,
    w_out,
    vec_first,
    vec_second,
    bias_first,
    bias_second,
    in_first,
    in_second,
    out_first,
    out_second,
):
    low = jnp.bfloat16
    mp = lax.axis_index("mp")
    small = jnp.zeros((8, 512), jnp.float32)
    small = small.at[:5, :SHARD].set(vectors).at[5, :UNIT].set(hidden_bias)
    x_all, cot_all, in_all, out_all, small_all = gather_all(
        inputs, cotangent, w_in.astype(low), w_out.astype(low), small
    )
    columns = jnp.transpose(small_all[:, :5, :SHARD], (0, 2, 1)).reshape(D, 5)
    gain_one, shift_one, gain_two, shift_two, out_bias = (columns[:, k : k + 1] for k in range(5))
    bias_all = small_all[:, 5, :UNIT].reshape(FF, 1)
    valid = local_valid(lengths, mp)[None, :]
    cos_d, sin_d = (jnp.asarray(t) for t in table(D))
    inputs_f = x_all.astype(jnp.float32)
    masked = (inputs_f * valid).astype(low)
    part_a = dot(cos_d, masked).astype(low)
    part_b = dot(sin_d, masked).astype(low)
    mixed = jnp.concatenate(
        [
            dot(part_a[:, o : o + n], cos_t) - dot(part_b[:, o : o + n], sin_t)
            for o, n, cos_t, sin_t in split_tables()
        ],
        axis=1,
    )
    first_hat, first_scale = layer_norm(inputs_f + mixed)
    hidden = first_hat * gain_one + shift_one
    hidden_low = hidden.astype(low)
    pre_act = dot_tn(in_all, hidden_low) + bias_all
    activ_f, gelu_back = jax.vjp(exact_gelu, pre_act)
    activated = activ_f.astype(low)
    second_res = hidden + dot_tn(out_all, activated) + out_bias
    second_hat, second_scale = layer_norm(second_res)
    layer_out = (second_hat * gain_two + shift_two).astype(low)
    out_grad = cot_all.astype(jnp.float32)
    second_grad = norm_back(out_grad * gain_two, second_hat, second_scale)
    second_low = second_grad.astype(low)
    pre_grad = gelu_back(dot(out_all, second_low))[0]
    pre_low = pre_grad.astype(low)
    grad_out = dot_nt(activated, second_low).astype(low)
    grad_in = dot_nt(pre_low, hidden_low).astype(low)
    hidden_grad = dot(in_all, pre_low) + second_grad
    first_grad = norm_back(hidden_grad * gain_one, first_hat, first_scale)
    first_low = first_grad.astype(low)
    grad_a = jnp.concatenate(
        [dot(first_low[:, o : o + n], cos_t) for o, n, cos_t, _ in split_tables()], axis=1
    ).astype(low)
    grad_b = jnp.concatenate(
        [-dot(first_low[:, o : o + n], sin_t) for o, n, _, sin_t in split_tables()], axis=1
    ).astype(low)
    back = (first_grad + valid * (dot(cos_d, grad_a) + dot(sin_d, grad_b))).astype(low)
    split = (4, 2, 2, 2, QUARTER, D)
    layer_mine, back_mine, sum_in, sum_out = scatter_all(
        layer_out, back, grad_in.reshape(split), grad_out.reshape(split)
    )
    grad_small = jnp.concatenate(
        [
            jnp.sum(hidden_grad * first_hat, axis=1),
            jnp.sum(hidden_grad, axis=1),
            jnp.sum(out_grad * second_hat, axis=1),
            jnp.sum(out_grad, axis=1),
            jnp.sum(second_grad, axis=1),
            jnp.sum(pre_grad, axis=1),
        ]
    )
    grad_small = lax.psum(grad_small, ("dp", "mp"))
    grad_vec = lax.dynamic_slice(grad_small[: 5 * D].reshape(5, D), (0, mp * SHARD), (5, SHARD))
    grad_bias = lax.dynamic_slice(grad_small[5 * D :], (mp * UNIT,), (UNIT,))
    grad_in = sum_in.reshape(UNIT, D).astype(jnp.float32).T
    grad_out = sum_out.reshape(UNIT, D).astype(jnp.float32)
    squares = (
        jnp.sum(grad_vec * grad_vec)
        + jnp.sum(grad_bias * grad_bias)
        + jnp.sum(grad_in * grad_in)
        + jnp.sum(grad_out * grad_out)
    )
    grad_norm = jnp.sqrt(lax.psum(squares, "mp"))
    factor = CLIP_LIMIT / jnp.maximum(grad_norm, CLIP_LIMIT)
    vec_state = adam_step(vectors, grad_vec, vec_first, vec_second, factor, RATE_SMALL, 0.0)
    bias_state = adam_step(hidden_bias, grad_bias, bias_first, bias_second, factor, RATE_SMALL, 0.0)
    in_state = adam_step(w_in, grad_in, in_first, in_second, factor, RATE_IN, DECAY_RATE)
    out_state = adam_step(w_out, grad_out, out_first, out_second, factor, RATE_OUT, DECAY_RATE)
    return (
        layer_mine,
        back_mine.astype(jnp.float32),
        grad_norm,
        *vec_state,
        *bias_state,
        *in_state,
        *out_state,
    )


def solution(mesh):
    in_specs = (
        P("mp", "dp"),
        P("mp", "dp"),
        P("dp"),
        P(None, "mp"),
        P("mp"),
        P(None, "mp"),
        P("mp", None),
        P(None, "mp"),
        P(None, "mp"),
        P("mp"),
        P("mp"),
        P(None, "mp"),
        P(None, "mp"),
        P("mp", None),
        P("mp", None),
    )
    out_specs = (
        P("mp", "dp"),
        P("mp", "dp"),
        P(),
        P(None, "mp"),
        P(None, "mp"),
        P(None, "mp"),
        P("mp"),
        P("mp"),
        P("mp"),
        P(None, "mp"),
        P(None, "mp"),
        P(None, "mp"),
        P("mp", None),
        P("mp", None),
        P("mp", None),
    )
    fits = mesh.shape["mp"] == N_MP and mesh.shape["dp"] == N_DP
    body = token_shards if fits else shards
    return jax.shard_map(body, mesh=mesh, in_specs=in_specs, out_specs=out_specs, check_vma=False)
```

```python
import functools
import math

import jax
import jax.numpy as jnp
import numpy as np
from jax import lax
from jax.experimental import pallas as pl
from jax.experimental.pallas import tpu as pltpu
from jax.sharding import PartitionSpec as P

D = 768
UNITS = 8
LONG_LEN = 512
MID_LEN = 256
SHORT_LEN = 128
STEP = 3


EPS_NORM = 1e-05
EPS_ADAM = 1e-08
BETA_ONE = 0.5
BETA_TWO = 0.5
CLIP_LIMIT = 1.0
DECAY_RATE = 0.01
RATE_IN = 0.03
RATE_OUT = 0.015
RATE_SMALL = 0.2


def buckets():
    return ((LONG_LEN, UNITS), (MID_LEN, UNITS), (SHORT_LEN, 2 * UNITS))


def dft_block(rows_index, cols_index, length):
    product = rows_index[:, None] * cols_index[None, :] % length
    angles = product.astype(jnp.float32) * (2.0 * math.pi / length)
    scaling = 1.0 / math.sqrt(length)
    return (
        (jnp.cos(angles) * scaling).astype(jnp.bfloat16),
        (jnp.sin(angles) * scaling).astype(jnp.bfloat16),
    )


def bucket_table(length):
    indices = jnp.arange(length, dtype=jnp.int32)
    cos_tab, sin_tab = dft_block(indices, indices, length)
    return jnp.concatenate([cos_tab, -sin_tab], axis=1)


def valid_tokens(lengths):
    pieces = []
    first_slot = 0
    for length, number in buckets():
        position = jnp.arange(length, dtype=jnp.int32)
        chosen = lengths[first_slot : first_slot + number]
        pieces.append(
            (position[None, :] < chosen[:, None]).astype(jnp.float32).reshape(number * length)
        )
        first_slot += number
    return jnp.concatenate(pieces)


def sequence_mix(part_a, part_b):
    pieces = []
    offset = 0
    for length, number in buckets():
        stacked_tab = bucket_table(length)
        extent = length * number
        block_a = part_a[:, offset : offset + extent].reshape(-1, number, length)
        block_b = part_b[:, offset : offset + extent].reshape(-1, number, length)
        joined = jnp.concatenate([block_a, block_b], axis=2)
        mixed_rows = jnp.einsum(
            "dun,mn->dum", joined, stacked_tab, preferred_element_type=jnp.float32
        )
        pieces.append(mixed_rows.reshape(-1, extent))
        offset += extent
    return jnp.concatenate(pieces, axis=1)


def sequence_unmix(grad_low):
    pieces_a = []
    pieces_b = []
    offset = 0
    for length, number in buckets():
        stacked_tab = bucket_table(length)
        extent = length * number
        sliced = grad_low[:, offset : offset + extent].reshape(-1, number, length)
        joined = jnp.einsum("dum,mn->dun", sliced, stacked_tab, preferred_element_type=jnp.float32)
        pieces_a.append(joined[:, :, :length].reshape(-1, extent))
        pieces_b.append(joined[:, :, length:].reshape(-1, extent))
        offset += extent
    return (jnp.concatenate(pieces_a, axis=1), jnp.concatenate(pieces_b, axis=1))


def normalize(values, row_sum, row_sq):
    mean_val = row_sum / D
    variance = row_sq / D - mean_val * mean_val
    scaling = lax.rsqrt(variance + EPS_NORM)[None, :]
    return ((values - mean_val[None, :]) * scaling, scaling)


def exact_gelu(values):
    return jax.nn.gelu(values, approximate=False)


def adam_step(weight, grad, first_old, second_old, factor, rate, decay):
    clipped = grad * factor
    first_new = BETA_ONE * first_old + (1.0 - BETA_ONE) * clipped
    second_new = BETA_TWO * second_old + (1.0 - BETA_TWO) * clipped * clipped
    first_hat = first_new / (1.0 - BETA_ONE**STEP)
    second_hat = second_new / (1.0 - BETA_TWO**STEP)
    weight_new = weight - rate * (first_hat / (jnp.sqrt(second_hat) + EPS_ADAM) + decay * weight)
    return (first_new, second_new, weight_new)


def shards(
    inputs,
    cotangent,
    lengths,
    vectors,
    hidden_bias,
    w_in,
    w_out,
    vec_first,
    vec_second,
    bias_first,
    bias_second,
    in_first,
    in_second,
    out_first,
    out_second,
):
    width_local = inputs.shape[0]
    group_tok = inputs.shape[1]
    feat_index = lax.axis_index("mp") * width_local + jnp.arange(width_local, dtype=jnp.int32)
    contract_first = (((0,), (0,)), ((), ()))
    contract_last = (((1,), (1,)), ((), ()))
    valid = valid_tokens(lengths)
    inputs_f = inputs.astype(jnp.float32)
    masked = (inputs_f * valid[None, :]).astype(jnp.bfloat16)
    rows_index = jnp.arange(width_local * lax.axis_size("mp"), dtype=jnp.int32)
    cos_tab, sin_tab = dft_block(rows_index, feat_index, D)
    both_parts = lax.psum_scatter(
        jnp.concatenate(
            [
                jnp.dot(cos_tab, masked, preferred_element_type=jnp.float32),
                jnp.dot(sin_tab, masked, preferred_element_type=jnp.float32),
            ],
            axis=1,
        ),
        "mp",
        scatter_dimension=0,
        tiled=True,
    )
    part_a = both_parts[:, :group_tok].astype(jnp.bfloat16)
    part_b = both_parts[:, group_tok:].astype(jnp.bfloat16)
    mixed_rows = sequence_mix(part_a, part_b)
    first_res = inputs_f + mixed_rows
    first_sum, first_sq = (
        lax.psum(jnp.sum(first_res, axis=0).astype(jnp.bfloat16), "mp").astype(jnp.float32),
        lax.psum(jnp.sum(first_res * first_res, axis=0).astype(jnp.bfloat16), "mp").astype(
            jnp.float32
        ),
    )
    first_hat, first_scale = normalize(first_res, first_sum, first_sq)
    hidden = first_hat * vectors[0][:, None] + vectors[1][:, None]
    hidden_low = hidden.astype(jnp.bfloat16)
    hidden_all = lax.all_gather(hidden_low, "mp", axis=0, tiled=True)
    w_in_low = w_in.astype(jnp.bfloat16)
    w_out_low = w_out.astype(jnp.bfloat16)
    pre_act = (
        lax.dot_general(w_in_low, hidden_all, contract_first, preferred_element_type=jnp.float32)
        + hidden_bias[:, None]
    )
    activ_f, gelu_back = jax.vjp(exact_gelu, pre_act)
    activated = activ_f.astype(jnp.bfloat16)
    columns = w_out_low
    down_part = lax.psum_scatter(
        lax.dot_general(
            columns, activated, contract_first, preferred_element_type=jnp.float32
        ).astype(jnp.bfloat16),
        "mp",
        scatter_dimension=0,
        tiled=True,
    ).astype(jnp.float32)
    second_res = hidden + down_part + vectors[4][:, None]
    second_sum, second_sq = (
        lax.psum(jnp.sum(second_res, axis=0).astype(jnp.bfloat16), "mp").astype(jnp.float32),
        lax.psum(jnp.sum(second_res * second_res, axis=0).astype(jnp.bfloat16), "mp").astype(
            jnp.float32
        ),
    )
    second_hat, second_scale = normalize(second_res, second_sum, second_sq)
    layer_out = (second_hat * vectors[2][:, None] + vectors[3][:, None]).astype(jnp.bfloat16)
    out_grad = cotangent.astype(jnp.float32)
    grad_gain_two = jnp.sum(out_grad * second_hat, axis=1)
    grad_shift_two = jnp.sum(out_grad, axis=1)
    scaled_two = out_grad * vectors[2][:, None]
    back_sum, back_dot = (
        lax.psum(jnp.sum(scaled_two, axis=0).astype(jnp.bfloat16), "mp").astype(jnp.float32),
        lax.psum(jnp.sum(scaled_two * second_hat, axis=0).astype(jnp.bfloat16), "mp").astype(
            jnp.float32
        ),
    )
    second_grad = second_scale * (
        scaled_two - back_sum[None, :] / D - second_hat * back_dot[None, :] / D
    )
    grad_out_bias = jnp.sum(second_grad, axis=1)
    second_low = second_grad.astype(jnp.bfloat16)
    row_block = lax.all_gather(second_low, "mp", axis=0, tiled=True)
    columns = w_out_low
    act_grad = jnp.dot(columns, row_block, preferred_element_type=jnp.float32)
    block_grad = lax.dot_general(
        activated, row_block, contract_last, preferred_element_type=jnp.float32
    )
    act_grad, grad_out = (act_grad, block_grad)
    pre_grad = gelu_back(act_grad)[0]
    grad_bias = jnp.sum(pre_grad, axis=1)
    pre_low = pre_grad.astype(jnp.bfloat16)
    grad_in = lax.dot_general(
        hidden_all, pre_low, contract_last, preferred_element_type=jnp.float32
    )
    row_block = w_in_low
    hidden_grad = (
        lax.psum_scatter(
            jnp.dot(row_block, pre_low, preferred_element_type=jnp.float32).astype(jnp.bfloat16),
            "mp",
            scatter_dimension=0,
            tiled=True,
        ).astype(jnp.float32)
        + second_grad
    )
    grad_gain_one = jnp.sum(hidden_grad * first_hat, axis=1)
    grad_shift_one = jnp.sum(hidden_grad, axis=1)
    scaled_one = hidden_grad * vectors[0][:, None]
    sum_one, dot_one = (
        lax.psum(jnp.sum(scaled_one, axis=0).astype(jnp.bfloat16), "mp").astype(jnp.float32),
        lax.psum(jnp.sum(scaled_one * first_hat, axis=0).astype(jnp.bfloat16), "mp").astype(
            jnp.float32
        ),
    )
    first_grad = first_scale * (
        scaled_one - sum_one[None, :] / D - first_hat * dot_one[None, :] / D
    )
    grad_a_f, grad_b_f = sequence_unmix(first_grad.astype(jnp.bfloat16))
    grad_a = grad_a_f.astype(jnp.bfloat16)
    grad_b = grad_b_f.astype(jnp.bfloat16)
    cols_index = jnp.arange(lax.axis_size("mp") * width_local, dtype=jnp.int32)
    cos_tab, sin_tab = dft_block(feat_index, cols_index, D)
    masked_grad = lax.psum_scatter(
        (
            lax.dot_general(cos_tab, grad_a, contract_first, preferred_element_type=jnp.float32)
            + lax.dot_general(sin_tab, grad_b, contract_first, preferred_element_type=jnp.float32)
        ).astype(jnp.bfloat16),
        "mp",
        scatter_dimension=0,
        tiled=True,
    ).astype(jnp.float32)
    input_grad = first_grad + valid[None, :] * masked_grad
    grad_vec = jnp.stack(
        [grad_gain_one, grad_shift_one, grad_gain_two, grad_shift_two, grad_out_bias]
    )
    grad_vec, grad_bias, grad_in, grad_out = (
        lax.psum(grad_vec.astype(jnp.bfloat16), "dp").astype(jnp.float32),
        lax.psum(grad_bias.astype(jnp.bfloat16), "dp").astype(jnp.float32),
        lax.psum(grad_in.astype(jnp.bfloat16), "dp").astype(jnp.float32),
        lax.psum(grad_out.astype(jnp.bfloat16), "dp").astype(jnp.float32),
    )
    squares = (
        jnp.sum(grad_vec * grad_vec)
        + jnp.sum(grad_bias * grad_bias)
        + jnp.sum(grad_in * grad_in)
        + jnp.sum(grad_out * grad_out)
    )
    total_sq = lax.psum(squares, "mp")
    grad_norm = jnp.sqrt(total_sq)
    factor = CLIP_LIMIT / jnp.maximum(grad_norm, CLIP_LIMIT)
    vec_state = adam_step(vectors, grad_vec, vec_first, vec_second, factor, RATE_SMALL, 0.0)
    bias_state = adam_step(hidden_bias, grad_bias, bias_first, bias_second, factor, RATE_SMALL, 0.0)
    in_state = adam_step(w_in, grad_in, in_first, in_second, factor, RATE_IN, DECAY_RATE)
    out_state = adam_step(w_out, grad_out, out_first, out_second, factor, RATE_OUT, DECAY_RATE)
    return (
        layer_out,
        input_grad,
        grad_norm,
        vec_state[0],
        vec_state[1],
        vec_state[2],
        bias_state[0],
        bias_state[1],
        bias_state[2],
        in_state[0],
        in_state[1],
        in_state[2],
        out_state[0],
        out_state[1],
        out_state[2],
    )


N_MP = 8
N_DP = 4
FF = 3072
SHARD = D // N_MP
UNIT = FF // N_MP
TOK = LONG_LEN + MID_LEN + 2 * SHORT_LEN
HALF = TOK // 2
QUARTER = UNIT // N_DP
ROWS_IN = D // N_DP
VMEM_LIMIT = 63 * 1024 * 1024
SLOTS = (
    ((UNITS * LONG_LEN, MID_LEN, 0), (UNITS * (LONG_LEN + MID_LEN), 2 * SHORT_LEN, MID_LEN)),
    ((0, LONG_LEN, HALF),),
)


def table(length):
    index = np.arange(length, dtype=np.int64)
    angles = ((index[:, None] * index[None, :]) % length).astype(np.float32) * np.float32(
        2.0 * math.pi / length
    )
    scaling = np.float32(1.0 / math.sqrt(length))
    return (
        (np.cos(angles).astype(np.float32) * scaling).astype(jnp.bfloat16),
        (np.sin(angles).astype(np.float32) * scaling).astype(jnp.bfloat16),
    )


def place():
    mp = lax.axis_index("mp")
    dp = lax.axis_index("dp")
    return mp, dp, mp // 2, mp % 2, dp // 2, dp % 2


def barrier():
    mp, dp = lax.axis_index("mp"), lax.axis_index("dp")
    sem = pltpu.get_barrier_semaphore()
    for step in range(1, N_MP):
        pl.semaphore_signal(sem, inc=1, device_id={"mp": (mp + step) % N_MP})
    for step in range(1, N_DP):
        pl.semaphore_signal(sem, inc=1, device_id={"dp": (dp + step) % N_DP})
    pl.semaphore_wait(sem, N_MP + N_DP - 2)


def wait_bytes(ref, sem):
    pltpu.make_async_copy(ref, ref, sem).wait()


def rows96(index):
    return pl.ds(pl.multiple_of(index * SHARD, 32), SHARD)


def spread_in(source, target, half, send_sem, recv_sem, own_sem):
    mp = lax.axis_index("mp")
    for offset, width, local in SLOTS[half]:
        for step in range(1, N_MP):
            peer = (mp + step) % N_MP
            pltpu.make_async_remote_copy(
                source.at[:, pl.ds(pl.multiple_of(offset + width * peer, 256), width)],
                target.at[rows96(mp), pl.ds(local, width)],
                send_sem,
                recv_sem,
                device_id={"mp": peer},
            ).start()
        pltpu.make_async_copy(
            source.at[:, pl.ds(pl.multiple_of(offset + width * mp, 256), width)],
            target.at[rows96(mp), pl.ds(local, width)],
            own_sem,
        ).start()


def spread_out(source, target, half, send_sem, recv_sem, own_sem):
    mp = lax.axis_index("mp")
    for offset, width, local in SLOTS[half]:
        columns = pl.ds(pl.multiple_of(offset + width * mp, 256), width)
        for step in range(1, N_MP):
            peer = (mp + step) % N_MP
            pltpu.make_async_remote_copy(
                source.at[rows96(peer), pl.ds(local, width)],
                target.at[:, columns],
                send_sem,
                recv_sem,
                device_id={"mp": peer},
            ).start()
        pltpu.make_async_copy(
            source.at[rows96(mp), pl.ds(local, width)], target.at[:, columns], own_sem
        ).start()


def region(ref, kind, mp, dp):
    if kind == 0:
        return ref.at[
            pl.ds(pl.multiple_of(dp * ROWS_IN, 64), ROWS_IN),
            pl.ds(pl.multiple_of(mp * UNIT, 128), UNIT),
        ]
    return ref.at[pl.ds(pl.multiple_of(mp * UNIT + dp * QUARTER, 32), QUARTER), :]


def push(ref, kind, mp, dp, target, send_sem, recv_sem):
    part = region(ref, kind, mp, dp)
    return pltpu.make_async_remote_copy(
        part, part, send_sem.at[kind], recv_sem.at[kind, mp * N_DP + dp], device_id=target
    )


def gather_steps(ref, kind, send_sem, recv_sem):
    mp, dp, z, x, y, c = place()

    def send(mp_from, dp_from, target):
        push(ref, kind, mp_from, dp_from, target, send_sem, recv_sem).start()

    def wait(mp_from, dp_from):
        push(ref, kind, mp_from, dp_from, {"mp": mp}, send_sem, recv_sem).wait_recv()

    to_x = {"mp": 2 * z + 1 - x}
    to_y = {"dp": 2 * (1 - y) + c}
    to_c = {"dp": 2 * y + 1 - c}

    def along_z():
        for step in range(1, 4):
            send(mp, dp, {"mp": 2 * ((z + step) % 4) + x})

    def second():
        if kind == 0:
            send(mp, dp, to_x)
        else:
            send(mp, dp, to_x)
            send(mp, 2 * (1 - y) + c, to_x)
        for step in range(1, 4):
            other = 2 * ((z + step) % 4) + x
            wait(other, dp)
            send(other, dp, to_x if kind == 0 else to_y)
            if kind == 0:
                send(other, dp, to_y)
            else:
                send(other, dp, to_x)

    def third():
        if kind == 0:
            for step in range(4):
                other = 2 * ((z + step) % 4) + 1 - x
                wait(other, dp)
                send(other, dp, to_y)
        else:
            for step in range(1, 4):
                other = 2 * ((z + step) % 4) + x
                wait(other, 2 * (1 - y) + c)
                send(other, 2 * (1 - y) + c, to_x)

    def fourth():
        for step in range(1, 4):
            other = 2 * ((z + step) % 4) + x
            send(other, dp, to_c)
        if kind == 0:
            for step in range(4):
                send(2 * ((z + step) % 4) + 1 - x, dp, to_c)
            for step in range(1, N_MP):
                other = (mp + step) % N_MP
                wait(other, 2 * (1 - y) + c)
                send(other, 2 * (1 - y) + c, to_c)
        else:
            for step in range(1, 4):
                send(2 * ((z + step) % 4) + x, 2 * (1 - y) + c, to_c)
            for half in (y, 1 - y):
                for step in range(4):
                    other = 2 * ((z + step) % 4) + 1 - x
                    wait(other, 2 * half + c)
                    send(other, 2 * half + c, to_c)

    def fifth():
        for half in (0, 1):
            for step in range(1, N_MP):
                wait((mp + step) % N_MP, 2 * half + 1 - c)

    return along_z, second, third, fourth, fifth


def add_into(ref, left, right):
    ref[...] = (left.astype(jnp.float32) + right.astype(jnp.float32)).astype(ref.dtype)


def reduce_steps(grad, kind, core_buf, second_buf, third_buf, last_buf, final, send, recv):
    mp, dp, z, x, y, c = place()
    to_x = {"mp": 2 * z + 1 - x}
    to_y = {"dp": 2 * (1 - y) + c}
    to_c = {"dp": 2 * y + 1 - c}

    def copy(stage, piece, source, target, device):
        return pltpu.make_async_remote_copy(
            source, target, send.at[kind, stage], recv.at[kind, stage, piece], device_id=device
        )

    def core(step):
        piece = (z + 1 + step) % 4
        return copy(0, step, grad.at[piece, :, :, 1 - c], core_buf.at[piece], to_c)

    def second(step):
        piece = (z + 1 + step) % 4
        if kind == 0:
            return copy(1, step, core_buf.at[piece, 1 - x], second_buf.at[piece], to_x)
        return copy(1, step, core_buf.at[piece, :, 1 - y], second_buf.at[piece], to_y)

    def third(step):
        piece = (z + 1 + step) % 4
        if kind == 0:
            return copy(2, step, second_buf.at[piece, 1 - y], third_buf.at[piece], to_y)
        return copy(2, step, second_buf.at[piece, 1 - x], third_buf.at[piece], to_x)

    def last(step):
        piece = (z + 1 + step) % 4
        return copy(3, step, third_buf.at[piece], last_buf.at[2 - step], {"mp": 2 * piece + x})

    def start(step):
        core(step).start()

    def after_core(step):
        piece = (z + 1 + step) % 4
        core(step).wait_recv()
        add_into(core_buf.at[piece], core_buf[piece], grad[piece, :, :, c])
        second(step).start()

    def after_second(step):
        piece = (z + 1 + step) % 4
        second(step).wait_recv()
        mine = core_buf[piece, x] if kind == 0 else core_buf[piece, :, y]
        add_into(second_buf.at[piece], second_buf[piece], mine)
        third(step).start()

    def after_third(step):
        piece = (z + 1 + step) % 4
        third(step).wait_recv()
        mine = second_buf[piece, y] if kind == 0 else second_buf[piece, x]
        add_into(third_buf.at[piece], third_buf[piece], mine)
        if step < 3:
            last(step).start()

    def finish():
        total = third_buf[z].astype(jnp.float32)
        for slot in range(3):
            pltpu.make_async_remote_copy(
                third_buf.at[z], last_buf.at[slot], send.at[kind, 3], recv.at[kind, 3, 2 - slot],
                device_id={"mp": mp},
            ).wait_recv()
            total = total + last_buf[slot].astype(jnp.float32)
        final[dp] = total.astype(final.dtype)
        for step in range(1, N_DP):
            pltpu.make_async_remote_copy(
                final.at[dp], final.at[dp], send.at[kind, 4], recv.at[kind, 4, 3 - step],
                device_id={"dp": (dp + step) % N_DP},
            ).start()

    def collect():
        for step in range(1, N_DP):
            other = (dp + N_DP - step) % N_DP
            pltpu.make_async_remote_copy(
                final.at[other], final.at[other], send.at[kind, 4], recv.at[kind, 4, 3 - step],
                device_id={"mp": mp},
            ).wait_recv()

    def drain():
        wait_bytes(core_buf, send.at[kind, 0])
        wait_bytes(second_buf, send.at[kind, 1])
        wait_bytes(third_buf, send.at[kind, 2])
        wait_bytes(third_buf.at[pl.ds(0, 3)], send.at[kind, 3])
        wait_bytes(final.at[pl.ds(0, 3)], send.at[kind, 4])

    return start, after_core, after_second, after_third, finish, collect, drain


def split_tables():
    cos_m, sin_m = table(MID_LEN)
    cos_s, sin_s = table(SHORT_LEN)
    cos_l, sin_l = table(LONG_LEN)
    zero = np.zeros_like(cos_s)
    cos_s = np.block([[cos_s, zero], [zero, cos_s]])
    sin_s = np.block([[sin_s, zero], [zero, sin_s]])
    return cos_m, sin_m, cos_s, sin_s, cos_l, sin_l


def local_valid(lengths, mp):
    def one(length, first, number):
        position = jnp.arange(length, dtype=jnp.int32)
        local = lax.dynamic_slice(lengths, (first + number * mp,), (number,))
        return (position[None, :] < local[:, None]).astype(jnp.float32).reshape(-1)

    return jnp.concatenate(
        [
            one(MID_LEN, UNITS, 1),
            one(SHORT_LEN, 2 * UNITS, 2),
            one(LONG_LEN, 0, 1),
        ]
    )


LOW = jnp.bfloat16
F32 = jnp.float32
BLOCK = D // 2
PIECES = (4, 2, 2, 2, QUARTER, D)
ERF_P = 0.44
ERF_C = (
    0.24821656338842543,
    0.24893493461024502,
    0.21693770822604325,
    0.2169836662829484,
    -0.022275437297594083,
    0.2988464364415672,
    -0.2791404617951606,
    0.0714967753199588,
)


def dot(left, right):
    return jnp.dot(left, right, preferred_element_type=F32)


def dot_nt(left, right):
    return lax.dot_general(left, right, (((1,), (1,)), ((), ())), preferred_element_type=F32)


def loop(count, step):
    def run(index, carry):
        step(index)
        return carry

    lax.fori_loop(0, count, run, 0)


def gelu_pair(value):
    size = jnp.abs(value)
    t = 1.0 / (1.0 + (ERF_P * math.sqrt(0.5)) * size)
    poly = 0.5 * ERF_C[-1]
    for coefficient in ERF_C[-2::-1]:
        poly = poly * t + 0.5 * coefficient
    bell = jnp.exp(-0.5 * (value * value))
    tail = poly * t * bell
    cdf = jnp.where(value < 0.0, tail, 1.0 - tail)
    return value * cdf, cdf + value * (bell * (1.0 / math.sqrt(2.0 * math.pi)))


def add_column(ref, index, column):
    lane = lax.broadcasted_iota(jnp.int32, ref.shape, 1)
    ref[...] += jnp.where(lane == index, column, 0.0)


class Refs:
    def __init__(self, names, refs):
        for name, ref in zip(names, refs, strict=True):
            setattr(self, name, ref)


INPUTS = (
    "inputs", "cotangent", "shard_in", "shard_out", "small", "valid",
    "cos_d", "sin_d", "cos_m", "sin_m", "cos_s", "sin_s", "cos_l", "sin_l",
)
OUTPUTS = ("layer_all", "back_all", "final_in", "final_out", "sum_vec", "sum_bias", "norm")
SCRATCH = {
    "w_in": pltpu.VMEM((D, FF), LOW),
    "w_out": pltpu.VMEM((FF, D), LOW),
    "turned_in": pltpu.VMEM(PIECES, LOW),
    "turned_out": pltpu.VMEM(PIECES, LOW),
    "x": pltpu.VMEM((D, TOK), LOW),
    "cot": pltpu.VMEM((D, TOK), LOW),
    "first": pltpu.VMEM((D, TOK), F32),
    "second": pltpu.VMEM((D, TOK), F32),
    "hidden_low": pltpu.VMEM((D, TOK), LOW),
    "second_low": pltpu.VMEM((D, TOK), LOW),
    "activ": pltpu.VMEM((FF, TOK), LOW),
    "slope": pltpu.VMEM((FF, TOK), LOW),
    "part_a": pltpu.VMEM((D, HALF), LOW),
    "part_b": pltpu.VMEM((D, HALF), LOW),
    "scales": pltpu.VMEM((16, TOK), F32),
    "columns": pltpu.VMEM((D, 128), F32),
    "bias": pltpu.VMEM((UNIT, 128), F32),
    "small_all": pltpu.VMEM((N_MP, 8, 512), F32),
    "unit": pltpu.VMEM((BLOCK, BLOCK), LOW),
    "t_cos_d": pltpu.VMEM((D, D), LOW),
    "t_sin_d": pltpu.VMEM((D, D), LOW),
    "t_cos_m": pltpu.VMEM((MID_LEN, MID_LEN), LOW),
    "t_sin_m": pltpu.VMEM((MID_LEN, MID_LEN), LOW),
    "t_cos_s": pltpu.VMEM((MID_LEN, MID_LEN), LOW),
    "t_sin_s": pltpu.VMEM((MID_LEN, MID_LEN), LOW),
    "t_cos_l": pltpu.VMEM((LONG_LEN, LONG_LEN), LOW),
    "t_sin_l": pltpu.VMEM((LONG_LEN, LONG_LEN), LOW),
    "core_in": pltpu.VMEM((4, 2, 2, QUARTER, D), LOW),
    "core_out": pltpu.VMEM((4, 2, 2, QUARTER, D), LOW),
    "second_in": pltpu.VMEM((4, 2, QUARTER, D), LOW),
    "second_out": pltpu.VMEM((4, 2, QUARTER, D), LOW),
    "third_in": pltpu.VMEM((4, QUARTER, D), LOW),
    "third_out": pltpu.VMEM((4, QUARTER, D), LOW),
    "last_in": pltpu.VMEM((3, QUARTER, D), LOW),
    "last_out": pltpu.VMEM((3, QUARTER, D), LOW),
    "grad_vec": pltpu.VMEM((D, 128), F32),
    "grad_bias": pltpu.VMEM((UNIT, 128), F32),
    "rows_bias": pltpu.VMEM((N_MP, 8, UNIT), F32),
    "mp_vec": pltpu.VMEM((N_MP, SHARD, 128), F32),
    "mp_bias": pltpu.VMEM((N_MP, 8, UNIT), F32),
    "dp_vec": pltpu.VMEM((N_DP, SHARD, 128), F32),
    "dp_bias": pltpu.VMEM((N_DP, 8, UNIT), F32),
    "squares": pltpu.VMEM((N_MP, 8, 128), F32),
    "send": pltpu.SemaphoreType.DMA((9,)),
    "recv": pltpu.SemaphoreType.DMA((9,)),
    "own": pltpu.SemaphoreType.DMA((9,)),
    "w_send": pltpu.SemaphoreType.DMA((2,)),
    "w_recv": pltpu.SemaphoreType.DMA((2, N_MP * N_DP)),
    "g_send": pltpu.SemaphoreType.DMA((2, 5)),
    "g_recv": pltpu.SemaphoreType.DMA((2, 5, 4)),
    "s_send": pltpu.SemaphoreType.DMA((5,)),
    "s_recv": pltpu.SemaphoreType.DMA((5,)),
    "load": pltpu.SemaphoreType.DMA((10,)),
}
TABLES = ("cos_d", "sin_d", "cos_m", "sin_m", "cos_s", "sin_s", "cos_l", "sin_l")


def groups(r, half):
    if half == 0:
        return (
            (0, MID_LEN, r.t_cos_m, r.t_sin_m),
            (MID_LEN, MID_LEN, r.t_cos_s, r.t_sin_s),
        )
    return ((0, LONG_LEN, r.t_cos_l, r.t_sin_l),)


def turn_small(r):
    for j in range(N_MP):
        block = jnp.concatenate(
            [r.small_all[j, :, 0:128], jnp.zeros((120, 128), F32)], axis=0
        )
        r.columns[pl.ds(j * SHARD, SHARD), :] = jnp.transpose(block)[:SHARD]
    rows = jnp.concatenate(
        [r.small_all[j, 5:6, 0:UNIT] for j in range(N_MP)] + [jnp.zeros((120, UNIT), F32)], axis=0
    )
    r.bias[...] = jnp.transpose(rows)


def unit_matrix(r):
    row = lax.broadcasted_iota(jnp.int32, r.unit.shape, 0)
    column = lax.broadcasted_iota(jnp.int32, r.unit.shape, 1)
    r.unit[...] = jnp.where(row == column, 1.0, 0.0).astype(LOW)


def column_of(ref, index):
    lane = lax.broadcasted_iota(jnp.int32, ref.shape, 1)
    return jnp.sum(jnp.where(lane == index, ref[...], 0.0), axis=1, keepdims=True)


def lanes(start, width):
    return pl.ds(pl.multiple_of(start, 128), width)


def mix(r, half):
    cols = pl.ds(half * HALF, HALF)
    r.hidden_low[:, cols] = (r.x[:, cols].astype(F32) * r.valid[0:1, cols]).astype(LOW)
    r.part_a[...] = dot(r.t_cos_d[...], r.hidden_low[:, cols]).astype(LOW)
    r.part_b[...] = dot(r.t_sin_d[...], r.hidden_low[:, cols]).astype(LOW)
    for start, width, cos_t, sin_t in groups(r, half):
        there = pl.ds(half * HALF + start, width)
        r.first[:, there] = (
            r.x[:, there].astype(F32)
            + dot(r.part_a[:, pl.ds(start, width)], cos_t[...])
            - dot(r.part_b[:, pl.ds(start, width)], sin_t[...])
        )

    def norm(step):
        there = lanes(half * HALF + step * 256, 256)
        values = r.first[:, there]
        mean_val = jnp.sum(values, axis=0, keepdims=True) * (1.0 / D)
        centred = values - mean_val
        variance = jnp.sum(centred * centred, axis=0, keepdims=True) * (1.0 / D)
        scaling = lax.rsqrt(variance + EPS_NORM)
        hat = centred * scaling
        r.first[:, there] = hat
        r.scales[0:1, there] = scaling
        r.hidden_low[:, there] = (hat * r.columns[:, 0:1] + r.columns[:, 1:2]).astype(LOW)

    loop(2, norm)


def turn_in(r):
    def step(index):
        block, side = index // 2, index % 2
        turned = dot_nt(r.unit[...], r.w_in[:, lanes(index * BLOCK, BLOCK)])
        r.turned_in[block, side] = turned.astype(LOW).reshape(2, 2, QUARTER, D)

    loop(8, step)


def turn_out(r):
    def step(index):
        rows = pl.ds(pl.multiple_of(index * D, 128), D)
        for side in range(2):
            turned = dot_nt(r.unit[...], r.w_out[rows, pl.ds(side * BLOCK, BLOCK)])
            r.turned_out[index, side] = turned.astype(LOW).reshape(2, 2, QUARTER, D)

    loop(4, step)


def up(r, half):
    cols = pl.ds(half * HALF, HALF)

    def step(index):
        block, side = index // 2, index % 2
        weights = r.turned_in[block, side].reshape(BLOCK, D)
        pre_act = dot(weights, r.hidden_low[:, cols]) + column_of(r.bias, index)
        value, slope = gelu_pair(pre_act)
        rows = pl.ds(pl.multiple_of(index * BLOCK, 128), BLOCK)
        r.activ[rows, cols] = value.astype(LOW)
        r.slope[rows, cols] = slope.astype(LOW)

    loop(8, step)


def down(r, half):
    cols = pl.ds(half * HALF, HALF)
    for side in range(2):
        rows = pl.ds(side * BLOCK, BLOCK)
        total = (
            r.first[rows, cols] * r.columns[rows, 0:1]
            + r.columns[rows, 1:2]
            + r.columns[rows, 4:5]
        )
        for block in range(4):
            total = total + dot(
                r.turned_out[block, side].reshape(BLOCK, D), r.activ[pl.ds(block * D, D), cols]
            )
        r.second[rows, cols] = total

    def norm(step):
        there = lanes(half * HALF + step * 256, 256)
        values = r.second[:, there]
        mean_val = jnp.sum(values, axis=0, keepdims=True) * (1.0 / D)
        centred = values - mean_val
        variance = jnp.sum(centred * centred, axis=0, keepdims=True) * (1.0 / D)
        scaling = lax.rsqrt(variance + EPS_NORM)
        hat = centred * scaling
        r.second[:, there] = hat
        r.scales[8:9, there] = scaling
        r.x[:, there] = (hat * r.columns[:, 2:3] + r.columns[:, 3:4]).astype(LOW)

    loop(2, norm)


def second_back(r, half):
    def step(index):
        there = lanes(half * HALF + index * 256, 256)
        out_grad = r.cot[:, there].astype(F32)
        hat = r.second[:, there]
        add_column(r.grad_vec, 2, jnp.sum(out_grad * hat, axis=1, keepdims=True))
        add_column(r.grad_vec, 3, jnp.sum(out_grad, axis=1, keepdims=True))
        scaled = out_grad * r.columns[:, 2:3]
        mean_grad = jnp.sum(scaled, axis=0, keepdims=True) * (1.0 / D)
        mean_dot = jnp.sum(scaled * hat, axis=0, keepdims=True) * (1.0 / D)
        grad = r.scales[8:9, there] * (scaled - mean_grad - hat * mean_dot)
        add_column(r.grad_vec, 4, jnp.sum(grad, axis=1, keepdims=True))
        r.second[:, there] = grad
        r.second_low[:, there] = grad.astype(LOW)

    loop(2, step)


def up_back(r, half):
    cols = pl.ds(half * HALF, HALF)

    def step(index):
        rows = pl.ds(pl.multiple_of(index * BLOCK, 128), BLOCK)
        act_grad = dot(r.w_out[rows, :], r.second_low[:, cols])
        pre_grad = act_grad * r.slope[rows, cols].astype(F32)
        add_column(r.grad_bias, index, jnp.sum(pre_grad, axis=1, keepdims=True))
        r.slope[rows, cols] = pre_grad.astype(LOW)

    loop(8, step)


def weight_grad(target, left, right, piece):
    def step(side):
        rows = pl.ds(pl.multiple_of((2 * piece + side) * BLOCK, 128), BLOCK)
        grad = dot_nt(left[rows, :], right[...])
        target[piece, side] = grad.astype(LOW).reshape(2, 2, QUARTER, D)

    loop(2, step)


def first_back(r, half):
    cols = pl.ds(half * HALF, HALF)
    for side in range(2):
        rows = pl.ds(side * BLOCK, BLOCK)
        r.second[rows, cols] += dot(r.w_in[rows, :], r.slope[:, cols])

    def step(index):
        there = lanes(half * HALF + index * 256, 256)
        grad = r.second[:, there]
        hat = r.first[:, there]
        add_column(r.grad_vec, 0, jnp.sum(grad * hat, axis=1, keepdims=True))
        add_column(r.grad_vec, 1, jnp.sum(grad, axis=1, keepdims=True))
        scaled = grad * r.columns[:, 0:1]
        mean_grad = jnp.sum(scaled, axis=0, keepdims=True) * (1.0 / D)
        mean_dot = jnp.sum(scaled * hat, axis=0, keepdims=True) * (1.0 / D)
        first_grad = r.scales[0:1, there] * (scaled - mean_grad - hat * mean_dot)
        r.first[:, there] = first_grad
        r.second_low[:, there] = first_grad.astype(LOW)

    loop(2, step)
    for start, width, cos_t, sin_t in groups(r, half):
        there, here = pl.ds(half * HALF + start, width), pl.ds(start, width)
        r.part_a[:, here] = dot(r.second_low[:, there], cos_t[...]).astype(LOW)
        r.part_b[:, here] = (-dot(r.second_low[:, there], sin_t[...])).astype(LOW)
    spread = dot(r.t_cos_d[...], r.part_a[...]) + dot(r.t_sin_d[...], r.part_b[...])
    r.cot[:, cols] = (r.first[:, cols] + r.valid[0:1, cols] * spread).astype(LOW)


def small_steps(r):
    mp, dp = lax.axis_index("mp"), lax.axis_index("dp")

    def over(axis, count, me, items, slot):
        for source, target in items:
            for step in range(1, count):
                peer = (me + step) % count
                pltpu.make_async_remote_copy(
                    source(peer), target.at[me], r.s_send.at[slot], r.s_recv.at[slot],
                    device_id={axis: peer},
                ).start()
            slot += 1

    def took(target, count, slot):
        wait_bytes(target.at[pl.ds(0, count - 1)], r.s_recv.at[slot])

    def to_mp():
        turned = jnp.transpose(r.grad_bias[...])
        for j in range(N_MP):
            r.rows_bias[j] = jnp.broadcast_to(turned[j : j + 1], (8, UNIT))
        own = rows96(mp)
        r.mp_vec[mp] = r.grad_vec[own, :]
        r.mp_bias[mp] = r.rows_bias[mp]
        items = (
            (lambda peer: r.grad_vec.at[rows96(peer), :], r.mp_vec),
            (lambda peer: r.rows_bias.at[peer], r.mp_bias),
        )
        over("mp", N_MP, mp, items, 0)

    def to_dp():
        took(r.mp_vec, N_MP, 0)
        took(r.mp_bias, N_MP, 1)
        r.dp_vec[dp] = jnp.sum(r.mp_vec[...], axis=0)
        r.dp_bias[dp] = jnp.sum(r.mp_bias[...], axis=0)
        items = (
            (lambda peer: r.dp_vec.at[dp], r.dp_vec),
            (lambda peer: r.dp_bias.at[dp], r.dp_bias),
        )
        over("dp", N_DP, dp, items, 2)

    def sums():
        took(r.dp_vec, N_DP, 2)
        took(r.dp_bias, N_DP, 3)
        r.sum_vec[...] = jnp.sum(r.dp_vec[...], axis=0)
        r.sum_bias[...] = jnp.sum(r.dp_bias[...], axis=0)

    def norm():
        def square(values):
            values = values.astype(F32)
            return jnp.sum(values * values)

        total = square(r.sum_vec[...]) + square(r.sum_bias[0:1, :])
        for quarter in range(N_DP):
            total = total + square(r.final_in[quarter]) + square(r.final_out[quarter])
        r.squares[mp] = jnp.full((8, 128), total, F32)
        over("mp", N_MP, mp, ((lambda peer: r.squares.at[mp], r.squares),), 4)
        took(r.squares, N_MP, 4)
        r.norm[...] = jnp.sum(r.squares[...], axis=0)

    def drain():
        wait_bytes(r.mp_vec.at[pl.ds(0, N_MP - 1)], r.s_send.at[0])
        wait_bytes(r.mp_bias.at[pl.ds(0, N_MP - 1)], r.s_send.at[1])
        wait_bytes(r.dp_vec.at[pl.ds(0, N_DP - 1)], r.s_send.at[2])
        wait_bytes(r.dp_bias.at[pl.ds(0, N_DP - 1)], r.s_send.at[3])
        wait_bytes(r.squares.at[pl.ds(0, N_MP - 1)], r.s_send.at[4])

    return to_mp, to_dp, sums, norm, drain


def step_kernel(*refs):
    r = Refs(INPUTS + OUTPUTS + tuple(SCRATCH), refs)
    mp = lax.axis_index("mp")
    shards = (
        pltpu.make_async_copy(r.shard_in, r.first.at[:, pl.ds(0, UNIT)], r.load.at[8]),
        pltpu.make_async_copy(r.shard_out, r.second.at[pl.ds(0, UNIT), pl.ds(0, D)], r.load.at[9]),
    )
    for copy in shards:
        copy.start()
    tables = [
        pltpu.make_async_copy(getattr(r, name), getattr(r, "t_" + name), r.load.at[slot])
        for slot, name in enumerate(TABLES)
    ]
    for copy in tables:
        copy.start()
    in_steps = gather_steps(r.w_in, 0, r.w_send, r.w_recv)
    out_steps = gather_steps(r.w_out, 1, r.w_send, r.w_recv)
    shards[0].wait()
    r.w_in[:, lanes(mp * UNIT, UNIT)] = r.first[:, pl.ds(0, UNIT)].astype(LOW)
    shards[1].wait()
    r.w_out[pl.ds(pl.multiple_of(mp * UNIT, 128), UNIT), :] = r.second[
        pl.ds(0, UNIT), pl.ds(0, D)
    ].astype(LOW)
    barrier()

    for step in range(1, N_MP):
        pltpu.make_async_remote_copy(
            r.small, r.small_all.at[mp], r.send.at[8], r.recv.at[8],
            device_id={"mp": (mp + step) % N_MP},
        ).start()
    own_small = pltpu.make_async_copy(r.small, r.small_all.at[mp], r.own.at[8])
    own_small.start()
    spread_in(r.inputs, r.x, 0, r.send.at[0], r.recv.at[0], r.own.at[0])
    in_steps[0]()
    out_steps[0]()
    spread_in(r.inputs, r.x, 1, r.send.at[1], r.recv.at[1], r.own.at[1])

    unit_matrix(r)
    r.grad_vec[...] = jnp.zeros_like(r.grad_vec)
    r.grad_bias[...] = jnp.zeros_like(r.grad_bias)
    wait_bytes(r.small_all.at[pl.ds(0, N_MP - 1)], r.recv.at[8])
    own_small.wait()
    turn_small(r)
    for copy in tables:
        copy.wait()

    def took_in(ref, half, slot):
        there = pl.ds(HALF * half, HALF)
        wait_bytes(ref.at[pl.ds(0, D - SHARD), there], r.recv.at[slot])
        wait_bytes(ref.at[pl.ds(0, SHARD), there], r.own.at[slot])

    in_steps[1]()
    out_steps[1]()
    took_in(r.x, 0, 0)
    spread_in(r.cotangent, r.cot, 0, r.send.at[2], r.recv.at[2], r.own.at[2])
    spread_in(r.cotangent, r.cot, 1, r.send.at[3], r.recv.at[3], r.own.at[3])
    mix(r, 0)
    in_steps[2]()
    out_steps[2]()
    in_steps[3]()
    out_steps[3]()
    took_in(r.x, 1, 1)
    mix(r, 1)
    in_steps[4]()
    turn_in(r)
    up(r, 0)
    up(r, 1)
    out_steps[4]()
    turn_out(r)
    for half in range(2):
        down(r, half)
        spread_out(
            r.x, r.layer_all, half, r.send.at[4 + half], r.recv.at[4 + half], r.own.at[4 + half]
        )
    for half in range(2):
        took_in(r.cot, half, 2 + half)
        second_back(r, half)
        up_back(r, half)

    outs = reduce_steps(
        r.turned_out, 1, r.core_out, r.second_out, r.third_out, r.last_out, r.final_out,
        r.g_send, r.g_recv,
    )
    ins = reduce_steps(
        r.turned_in, 0, r.core_in, r.second_in, r.third_in, r.last_in, r.final_in,
        r.g_send, r.g_recv,
    )
    tiny = small_steps(r)
    z = mp // 2
    for step in range(4):
        weight_grad(r.turned_out, r.activ, r.second_low, (z + 1 + step) % 4)
        outs[0](step)
    for step in range(4):
        weight_grad(r.turned_in, r.slope, r.hidden_low, (z + 1 + step) % 4)
        ins[0](step)
        outs[1](step)
    for half in range(2):
        first_back(r, half)
        spread_out(
            r.cot, r.back_all, half, r.send.at[6 + half], r.recv.at[6 + half], r.own.at[6 + half]
        )
        if half == 1:
            tiny[0]()
        for step in range(4):
            if half == 0:
                ins[1](step)
                outs[2](step)
            else:
                ins[2](step)
                outs[3](step)
    tiny[1]()
    for step in range(4):
        ins[3](step)
    outs[4]()
    tiny[2]()
    ins[4]()
    outs[5]()
    ins[5]()
    tiny[3]()

    tiny[4]()
    outs[6]()
    ins[6]()
    for kind in range(2):
        wait_bytes(r.w_out.at[pl.ds(0, 28 * QUARTER), :], r.w_send.at[kind])
    wait_bytes(r.small_all.at[pl.ds(0, N_MP - 1)], r.send.at[8])
    for slot in range(8):
        if slot >= 4:
            target = r.layer_all if slot < 6 else r.back_all
            wait_bytes(target.at[:, pl.ds(0, 7 * HALF)], r.recv.at[slot])
            wait_bytes(target.at[:, pl.ds(0, HALF)], r.own.at[slot])
        wait_bytes(r.x.at[pl.ds(0, D - SHARD), pl.ds(0, HALF)], r.send.at[slot])


def call_step(*operands):
    anywhere = pl.BlockSpec(memory_space=pl.ANY)
    vmem = pl.BlockSpec(memory_space=pltpu.VMEM)
    tokens = operands[0].shape[1]
    return pl.pallas_call(
        step_kernel,
        out_shape=(
            jax.ShapeDtypeStruct((SHARD, tokens), LOW),
            jax.ShapeDtypeStruct((SHARD, tokens), LOW),
            jax.ShapeDtypeStruct((N_DP, QUARTER, D), LOW),
            jax.ShapeDtypeStruct((N_DP, QUARTER, D), LOW),
            jax.ShapeDtypeStruct((SHARD, 128), F32),
            jax.ShapeDtypeStruct((8, UNIT), F32),
            jax.ShapeDtypeStruct((8, 128), F32),
        ),
        in_specs=[anywhere] * 5 + [vmem] + [anywhere] * 8,
        out_specs=(anywhere,) * 2 + (vmem,) * 5,
        scratch_shapes=list(SCRATCH.values()),
        compiler_params=pltpu.CompilerParams(
            collective_id=0, has_side_effects=True, vmem_limit_bytes=VMEM_LIMIT
        ),
    )(*operands)


def token_shards(
    inputs,
    cotangent,
    lengths,
    vectors,
    hidden_bias,
    w_in,
    w_out,
    vec_first,
    vec_second,
    bias_first,
    bias_second,
    in_first,
    in_second,
    out_first,
    out_second,
):
    mp = lax.axis_index("mp")
    small = jnp.concatenate(
        [
            jnp.pad(vectors, ((0, 0), (0, 512 - SHARD))),
            jnp.pad(hidden_bias[None, :], ((0, 2), (0, 512 - UNIT))),
        ],
        axis=0,
    )
    valid = jnp.broadcast_to(local_valid(lengths, mp)[None, :], (8, TOK))
    cos_m, sin_m, cos_s, sin_s, cos_l, sin_l = split_tables()
    tables = [jnp.asarray(t) for t in (*table(D), cos_m, sin_m, cos_s, sin_s, cos_l, sin_l)]
    layer_mine, back_mine, sum_in, sum_out, sum_vec, sum_bias, total_sq = call_step(
        inputs, cotangent, w_in, w_out, small, valid, *tables
    )
    grad_norm = jnp.sqrt(total_sq[0, 0])
    factor = CLIP_LIMIT / jnp.maximum(grad_norm, CLIP_LIMIT)
    grad_vec = sum_vec[:, :5].T
    grad_bias = sum_bias[0]
    grad_in = sum_in.reshape(UNIT, D).astype(jnp.float32).T
    grad_out = sum_out.reshape(UNIT, D).astype(jnp.float32)
    vec_state = adam_step(vectors, grad_vec, vec_first, vec_second, factor, RATE_SMALL, 0.0)
    bias_state = adam_step(hidden_bias, grad_bias, bias_first, bias_second, factor, RATE_SMALL, 0.0)
    in_state = adam_step(w_in, grad_in, in_first, in_second, factor, RATE_IN, DECAY_RATE)
    out_state = adam_step(w_out, grad_out, out_first, out_second, factor, RATE_OUT, DECAY_RATE)
    return (
        layer_mine,
        back_mine.astype(jnp.float32),
        grad_norm,
        *vec_state,
        *bias_state,
        *in_state,
        *out_state,
    )


def solution(mesh):
    in_specs = (
        P("mp", "dp"),
        P("mp", "dp"),
        P("dp"),
        P(None, "mp"),
        P("mp"),
        P(None, "mp"),
        P("mp", None),
        P(None, "mp"),
        P(None, "mp"),
        P("mp"),
        P("mp"),
        P(None, "mp"),
        P(None, "mp"),
        P("mp", None),
        P("mp", None),
    )
    out_specs = (
        P("mp", "dp"),
        P("mp", "dp"),
        P(),
        P(None, "mp"),
        P(None, "mp"),
        P(None, "mp"),
        P("mp"),
        P("mp"),
        P("mp"),
        P(None, "mp"),
        P(None, "mp"),
        P(None, "mp"),
        P("mp", None),
        P("mp", None),
        P("mp", None),
    )
    fits = mesh.shape["mp"] == N_MP and mesh.shape["dp"] == N_DP
    body = token_shards if fits else shards
    return jax.shard_map(body, mesh=mesh, in_specs=in_specs, out_specs=out_specs, check_vma=False)
```
